128 devices in a mesh: line: 16 (over x, y), blk: 8 (over z, core).
Axes of the slice: x: 4, y: 4, z: 4, core: 2. Of those that a mesh axis runs over, the one named last changes fastest.
Arguments:
- state: float32 [5, 512, 128, 128], P(None, 'line', 'blk'), may hold values from -6 to 6
- forcing: float32 [5, 512, 128, 128], P(None, 'line', 'blk'), may hold values from -6 to 6
- viscosity: float32 [5], replicated, may hold values from 0.05 to 0.3
- coupling: float32 [5, 5], replicated, may hold values from -2.5 to 2.5
- thrust: float32 [5], replicated, may hold values from 0.5 to 2
- disk_mask: int32 [512, 128, 128], P('line', 'blk'), may hold values 0 or 1
- block_inverse: float32 [5, 5, 512, 128, 128], P(None, None, 'line', 'blk'), may hold values from -0.12 to 1.4, as said below
- lower_decay: float32 [5, 512, 128, 128], P(None, 'line', 'blk'), may hold values from 0 to 1, as said below
- upper_decay: float32 [5, 512, 128, 128], P(None, 'line', 'blk'), may hold values from 0 to 1, as said below
Outputs:
- update: float32 [5, 512, 128, 128], P(None, 'line', 'blk')
- residual: float32 [5, 512, 128, 128], P(None, 'line', 'blk')
The draws below stay inside these ranges and needn't reach their ends.
Inputs may be any that keep to these rules, and one draw needn't show every extreme that they name: `block_inverse`: diagonal entries lie between 0.6 and 1.4, the others between -0.12 and 0.12. `lower_decay`: each entry lies strictly between 0 and 1. `upper_decay`: each entry lies strictly between 0 and 1.
All inputs are finite; a program needn't handle non-finite values. No bound on the sum of `disk_mask` on one device may be relied on, other than what follows from the above.
Results may differ from the reference program's by a relative error of at most 0.00023.
Values sent between devices are 32-bit elements; how exact they have to be, the bound alone decides.
A program may use at most 128 MiB of HBM per device.

```python
import math
import jax
import jax.numpy as jnp
from jax import lax

FIELDS = 5
NY = 128
NZ = 512
NX = 128


def draw_decay(key):
    rate_key, jitter_key, spot_key, depth_key = jax.random.split(key, 4)
    lowest = 0.3 / NZ
    highest = 1.0 / 30.0
    rate = jnp.exp(jax.random.uniform(rate_key, (FIELDS, 1, NX, NY), jnp.float32, math.log(lowest), math.log(highest)))
    jitter = jax.random.uniform(jitter_key, (FIELDS, NZ, NX, NY), jnp.float32, 0.5, 1.5)
    spots = jax.random.randint(spot_key, (3,), 0, NZ)
    struck = jnp.any(jnp.arange(NZ)[:, None] == spots[None, :], axis=1)
    depth = jax.random.uniform(depth_key, (FIELDS, NZ, NX, NY), jnp.float32, 0.5, 0.8)
    factor = jnp.where(struck[None, :, None, None], depth, 1.0)
    return jnp.exp(-rate * jitter) * factor


def draw_lower_decay(key, part):
    return draw_decay(jax.random.fold_in(key, 11))


def draw_upper_decay(key, part):
    return draw_decay(jax.random.fold_in(key, 23))


def draw_block_inverse(key, part):
    diag_key, off_key = jax.random.split(key)
    offdiag = jax.random.uniform(off_key, (FIELDS, FIELDS, NZ, NX, NY), jnp.float32, -0.12, 0.12)
    diagonal = jax.random.uniform(diag_key, (FIELDS, NZ, NX, NY), jnp.float32, 0.6, 1.4)
    eye = jnp.eye(FIELDS, dtype=jnp.float32)[:, :, None, None, None]
    return offdiag * (1.0 - eye) + eye * diagonal[None]


def draw_forcing(key, part):
    return jax.random.truncated_normal(key, -6.0, 6.0, (FIELDS, NZ, NX, NY), jnp.float32)


def place_ends(entries, own_key, low, high):
    longest = entries.shape.index(max(entries.shape))
    spots = []
    for shift in (0, 1):
        where = [jax.random.randint(jax.random.fold_in(own_key, axis), (), 0, length) for axis, length in enumerate(entries.shape)]
        where[longest] = (where[longest] + shift) % entries.shape[longest]
        spots.append(tuple(where))
    return entries.at[spots[0]].set(low).at[spots[1]].set(high)


def block_levels(own_key, shape, shards, smallest, high):
    def one(position, parts):
        steps = jax.random.uniform(jax.random.fold_in(jax.random.fold_in(own_key, 6), position), (parts,), jnp.float32, smallest / len(shards), high / len(shards))
        return jnp.repeat(jnp.exp(steps), shape[position] // parts).reshape((-1,) + (1,) * (len(shape) - position - 1))

    loudness = one(*shards[0])
    for cut in shards[1:]:
        loudness = loudness * one(*cut)
    return loudness


def normal_values(stream_key, extent, spread, bound, shards=(), kind=jnp.bfloat16):
    result = spread * jax.random.normal(stream_key, extent, jnp.float32)
    if shards:
        result = result * block_levels(stream_key, extent, shards, -0.22, 0.18)
    return jnp.clip(result, -bound, bound).astype(kind)


def setup_inputs(seed: int = 0) -> dict:
    key_of = jax.random.split(jax.random.key(seed), 10)
    return {
        "state": normal_values(key_of[0], (FIELDS, NZ, NX, NY), 1.0, 6.0, ((1, 16), (2, 8)), jnp.float32),
        "forcing": draw_forcing(jax.random.fold_in(key_of[9], 71), 0),
        "viscosity": jnp.clip(jnp.exp(jax.random.uniform(key_of[2], (FIELDS,), jnp.float32, math.log(0.05), math.log(0.3))), 0.05, 0.3),
        "coupling": normal_values(key_of[3], (FIELDS, FIELDS), FIELDS ** -0.5, 2.5, (), jnp.float32),
        "thrust": jnp.clip(jnp.exp(jax.random.uniform(key_of[4], (FIELDS,), jnp.float32, math.log(0.5), math.log(2.0))), 0.5, 2.0),
        "disk_mask": place_ends((jax.random.randint(key_of[5], (NZ, NX, NY), 0, 8) < 1).astype(jnp.int32), jax.random.fold_in(key_of[5], 1), 0, 1),
        "block_inverse": draw_block_inverse(jax.random.fold_in(key_of[9], 71), 0),
        "lower_decay": draw_lower_decay(jax.random.fold_in(key_of[9], 71), 0),
        "upper_decay": draw_upper_decay(jax.random.fold_in(key_of[9], 71), 0),
    }


def combine_maps(first, second):
    return (first[0] * second[0], second[0] * first[1] + second[1])

def mix(matrix, field):
    total = matrix[:, 0] * field[0]
    for index in range(1, field.shape[0]):
        total = total + matrix[:, index] * field[index]
    return total

def line_solve(source, lower, upper):
    swept = lax.associative_scan(combine_maps, (lower, jnp.sqrt(1.0 - lower * lower) * source), axis=1)[1]
    return lax.associative_scan(combine_maps, (upper, jnp.sqrt(1.0 - upper * upper) * swept), reverse=True, axis=1)[1]

def reference(state, forcing, viscosity, coupling, thrust, disk_mask, block_inverse, lower_decay, upper_decay):
    padded = jnp.pad(state, ((0, 0), (1, 1), (1, 1), (0, 0)))
    beside = padded[:, 2:, 1:-1] + padded[:, :-2, 1:-1] + padded[:, 1:-1, 2:] + padded[:, 1:-1, :-2]
    beside = beside + jnp.roll(state, 1, 3) + jnp.roll(state, -1, 3)
    diffusion = viscosity[:, None, None, None] * (6.0 * state - beside)
    sink = disk_mask.astype(jnp.float32)[None] * thrust[:, None, None, None] * state
    residual = forcing - diffusion - mix(coupling[:, :, None, None, None], state) - sink
    source = mix(block_inverse, residual)
    pieces = []
    for field in range(source.shape[0]):
        pieces.append(line_solve(source[field:field + 1], lower_decay[field:field + 1], upper_decay[field:field + 1]))
    update = jnp.concatenate(pieces, axis=0)
    return (update, residual)
```

```python
import jax
import jax.numpy as jnp
from jax import lax
from jax.experimental import pallas as pl
from jax.experimental.pallas import tpu as pltpu
from jax.sharding import PartitionSpec as P

F = 5
NV = 2 * F
CH = 4


def kernel(
    visc_h, coup_h, thr_h, state_h, forcing_h, mask_h, binv_h, lower_h, upper_h,
    update_h, resid_h,
    st, fo, mk, bi, lo, up, gl, gu, qg, rr, vv, sw,
    visc, coup, thr, xs, xh, acd_s, acd_r, be_s, be_r, ret_s, ret_r,
    load_sem, small_sem, chunk_sem, halo_ssem, halo_rsem,
    acd_ssem, acd_rsem, be_ssem, be_rsem, ret_ssem, ret_rsem, out_sem,
):
    n_line = lax.axis_size("line")
    n_blk = lax.axis_size("blk")
    me = lax.axis_index("line")
    mb = lax.axis_index("blk")
    depth = lo.shape[1]
    step = depth // CH

    def load(src, dst, sem):
        return pltpu.make_async_copy(src, dst, sem)

    ld_state = load(state_h, st.at[:, pl.ds(1, depth)], load_sem.at[0])
    ld_lower = load(lower_h, lo, load_sem.at[1])
    ld_upper = load(upper_h, up, load_sem.at[2])
    ld_small = [
        load(src, dst, small_sem.at[i])
        for i, (src, dst) in enumerate(((visc_h, visc), (coup_h, coup), (thr_h, thr)))
    ]
    ld_state.start()
    ld_lower.start()
    ld_upper.start()

    def chunk_loads(k):
        part = pl.ds(k * step, step)
        return (
            load(forcing_h.at[:, part], fo.at[:, part], chunk_sem.at[0, k]),
            load(mask_h.at[part], mk.at[part], chunk_sem.at[1, k]),
            load(binv_h.at[:, :, part], bi.at[:, :, part], chunk_sem.at[2, k]),
        )

    for cp in ld_small:
        cp.start()

    for k in range(CH):
        for cp in chunk_loads(k):
            cp.start()

    barrier = pltpu.get_barrier_semaphore()

    def greet(d, c):
        pl.semaphore_signal(barrier, inc=1, device_id={"line": lax.rem(me + d, n_line)})
        return c

    lax.fori_loop(1, n_line, greet, 0)

    @pl.when(mb > 0)
    def _():
        pl.semaphore_signal(barrier, inc=1, device_id={"blk": mb - 1})

    @pl.when(mb < n_blk - 1)
    def _():
        pl.semaphore_signal(barrier, inc=1, device_id={"blk": mb + 1})

    ld_state.wait()

    for c in range(F):
        for side, row in ((0, 0), (1, 15)):
            xs[side, c] = st[c, 1 : depth + 1, row, :]

    beside_blk = jnp.where(mb > 0, 1, 0) + jnp.where(mb < n_blk - 1, 1, 0)
    pl.semaphore_wait(barrier, n_line - 1 + beside_blk)

    def z_send(side):
        to = me - 1 if side == 0 else me + 1
        src = st.at[:, 1] if side == 0 else st.at[:, depth]
        dst = st.at[:, depth + 1] if side == 0 else st.at[:, 0]
        return pltpu.make_async_remote_copy(
            src_ref=src, dst_ref=dst, send_sem=halo_ssem.at[side], recv_sem=halo_rsem.at[side],
            device_id={"line": to},
        )

    def x_send(side):
        to = mb - 1 if side == 0 else mb + 1
        return pltpu.make_async_remote_copy(
            src_ref=xs.at[side], dst_ref=xh.at[1 - side],
            send_sem=halo_ssem.at[2 + side], recv_sem=halo_rsem.at[2 + side],
            device_id={"blk": to},
        )

    zeros_plane = jnp.zeros((F, 16, 128), jnp.float32)
    zeros_side = jnp.zeros((F, depth, 128), jnp.float32)

    @pl.when(mb > 0)
    def _():
        x_send(0).start()

    @pl.when(mb < n_blk - 1)
    def _():
        x_send(1).start()

    @pl.when(me > 0)
    def _():
        z_send(0).start()

    @pl.when(me < n_line - 1)
    def _():
        z_send(1).start()

    @pl.when(mb == 0)
    def _():
        xh[0] = zeros_side

    @pl.when(mb == n_blk - 1)
    def _():
        xh[1] = zeros_side

    @pl.when(me == 0)
    def _():
        st[:, 0] = zeros_plane

    @pl.when(me == n_line - 1)
    def _():
        st[:, depth + 1] = zeros_plane

    ld_lower.wait()
    ld_upper.wait()
    ones = jnp.ones((F, 16, 128), jnp.float32)

    def early_up(z, carry):
        p, q = carry
        l = lo[:, z]
        u = up[:, z]
        l2 = 1.0 - l * l
        u2 = 1.0 - u * u
        g = u2 * lax.rsqrt(u2)
        gl[:, z] = l2 * lax.rsqrt(l2)
        gu[:, z] = g
        p = p * l
        rr[:, z] = g * p
        qg[:, z] = q * g
        return p, q * u

    p_all, _ = lax.fori_loop(0, depth, early_up, (ones, ones))

    def early_down(i, carry):
        r, v = carry
        z = depth - 1 - i
        u = up[:, z]
        r = u * r + rr[:, z]
        v = u * v
        rr[:, z] = r
        vv[:, z] = v
        return r, v

    d_all, c_all = lax.fori_loop(0, depth, early_down, (jnp.zeros_like(ones), ones))

    for i, val in enumerate((p_all, c_all, d_all)):
        for c in range(F):
            for h in range(2):
                acd_s[2 * c + h, i] = val[c, 8 * h : 8 * h + 8]

    def acd_copy(j):
        return pltpu.make_async_remote_copy(
            src_ref=acd_s.at[j], dst_ref=acd_r.at[me], send_sem=acd_ssem.at[j], recv_sem=acd_rsem,
            device_id={"line": j},
        )

    def be_copy(j):
        return pltpu.make_async_remote_copy(
            src_ref=be_s.at[j], dst_ref=be_r.at[me], send_sem=be_ssem.at[j], recv_sem=be_rsem,
            device_id={"line": j},
        )

    def to_solvers(action):
        def one(d, c):
            j = lax.rem(me + d, n_line)

            @pl.when(j < NV)
            def _():
                action(j)

            return c

        lax.fori_loop(1, n_line, one, 0)

    to_solvers(lambda j: acd_copy(j).start())

    @pl.when(me < NV)
    def _():
        acd_r[me] = acd_s[me]

    @pl.when(mb > 0)
    def _():
        x_send(1).wait_recv()

    @pl.when(mb < n_blk - 1)
    def _():
        x_send(0).wait_recv()

    @pl.when(me > 0)
    def _():
        z_send(1).wait_recv()

    @pl.when(me < n_line - 1)
    def _():
        z_send(0).wait_recv()

    rows = lax.broadcasted_iota(jnp.int32, (8, 128), 0)
    first = rows == 0
    last = rows == 7
    for cp in ld_small:
        cp.wait()
    vis = [visc[c] for c in range(F)]
    thrust = [thr[c] for c in range(F)]
    mat = [[coup[c, d] + 6.0 * vis[c] if c == d else coup[c, d] for d in range(F)] for c in range(F)]

    def residual_copy(k):
        part = pl.ds(k * step, step)
        return pltpu.make_async_copy(fo.at[:, part], resid_h.at[:, part], out_sem.at[0, k])

    def cell(z, carry):
        s, e = carry
        cen = [[st[c, z + 1, 8 * h : 8 * h + 8, :] for h in range(2)] for c in range(F)]
        m = [mk[z, 8 * h : 8 * h + 8, :].astype(jnp.float32) for h in range(2)]
        res = []
        for c in range(F):
            v0, v1 = cen[c]
            r0, r1 = pltpu.roll(v0, 1, 0), pltpu.roll(v1, 1, 0)
            q0, q1 = pltpu.roll(v0, 7, 0), pltpu.roll(v1, 7, 0)
            before = jnp.broadcast_to(xh[0, c, pl.ds(z, 1), :], (8, 128))
            after = jnp.broadcast_to(xh[1, c, pl.ds(z, 1), :], (8, 128))
            xsum = (
                jnp.where(first, before, r0) + jnp.where(last, q1, q0),
                jnp.where(first, r0, r1) + jnp.where(last, after, q1),
            )
            pair = []
            for h in range(2):
                sub = slice(8 * h, 8 * h + 8)
                v = cen[c][h]
                beside = st[c, z, sub, :] + st[c, z + 2, sub, :]
                beside = beside + (pltpu.roll(v, 1, 1) + pltpu.roll(v, 127, 1))
                beside = beside + xsum[h]
                total = (mat[c][c] + m[h] * thrust[c]) * v
                for d in range(F):
                    if d != c:
                        total = total + mat[c][d] * cen[d][h]
                r = (fo[c, z, sub, :] + vis[c] * beside) - total
                fo[c, z, sub, :] = r
                pair.append(r)
            res.append(pair)
        new_s, new_e = [], []
        for c in range(F):
            for h in range(2):
                sub = slice(8 * h, 8 * h + 8)
                src = bi[c, 0, z, sub, :] * res[0][h]
                for d in range(1, F):
                    src = src + bi[c, d, z, sub, :] * res[d][h]
                v = lo[c, z, sub, :] * s[2 * c + h] + gl[c, z, sub, :] * src
                sw[c, z, sub, :] = v
                new_s.append(v)
                new_e.append(e[2 * c + h] + qg[c, z, sub, :] * v)
        return tuple(new_s), tuple(new_e)

    def chunk(k, carry):
        for cp in chunk_loads(k):
            cp.wait()
        carry = lax.fori_loop(k * step, (k + 1) * step, cell, carry)
        residual_copy(k).start()
        return carry

    zero = tuple(jnp.zeros((8, 128), jnp.float32) for _ in range(NV))
    b_all, e_all = lax.fori_loop(0, CH, chunk, (zero, zero))
    for v in range(NV):
        be_s[v, 0] = b_all[v]
        be_s[v, 1] = e_all[v]
    to_solvers(lambda j: be_copy(j).start())

    def ret_copy(k):
        return pltpu.make_async_remote_copy(
            src_ref=ret_s.at[k], dst_ref=ret_r.at[me], send_sem=ret_ssem.at[k], recv_sem=ret_rsem,
            device_id={"line": k},
        )

    @pl.when(me < NV)
    def _():
        be_r[me] = be_s[me]

    def back(i, u):
        z = depth - 1 - i
        u = up[:, z] * u + gu[:, z] * sw[:, z]
        sw[:, z] = u
        return u

    lax.fori_loop(0, depth, back, jnp.zeros_like(ones))

    def drain(ref, sem):
        pltpu.make_async_copy(ref, ref, sem).wait()

    @pl.when(me < NV)
    def _():
        drain(acd_r.at[pl.ds(0, n_line - 1)], acd_rsem)
        drain(be_r.at[pl.ds(0, n_line - 1)], be_rsem)
        s = jnp.zeros((8, 128), jnp.float32)
        t = []
        for k in range(n_line):
            ret_s[k, 0] = s
            t.append(acd_r[k, 2] * s + be_r[k, 1])
            s = acd_r[k, 0] * s + be_r[k, 0]
        u = jnp.zeros((8, 128), jnp.float32)
        for k in range(n_line - 1, -1, -1):
            ret_s[k, 1] = u
            u = acd_r[k, 1] * u + t[k]

        def answer(d, c):
            ret_copy(lax.rem(me + d, n_line)).start()
            return c

        lax.fori_loop(1, n_line, answer, 0)
        ret_r[me] = ret_s[me]
        drain(ret_r.at[pl.ds(0, NV - 1)], ret_rsem)

    @pl.when(me >= NV)
    def _():
        drain(ret_r.at[pl.ds(0, NV)], ret_rsem)

    def update_copy(k):
        part = pl.ds(k * step, step)
        return pltpu.make_async_copy(sw.at[:, part], update_h.at[:, part], out_sem.at[1, k])

    s_in = jnp.stack([jnp.concatenate([ret_r[2 * c, 0], ret_r[2 * c + 1, 0]], axis=0) for c in range(F)])
    u_in = jnp.stack([jnp.concatenate([ret_r[2 * c, 1], ret_r[2 * c + 1, 1]], axis=0) for c in range(F)])

    def finish(k, c):
        def one(z, c):
            sw[:, z] = sw[:, z] + rr[:, z] * s_in + vv[:, z] * u_in
            return c

        lax.fori_loop(k * step, (k + 1) * step, one, 0)
        update_copy(k).start()
        return c

    lax.fori_loop(0, CH, finish, 0)

    @pl.when(mb > 0)
    def _():
        x_send(0).wait_send()

    @pl.when(mb < n_blk - 1)
    def _():
        x_send(1).wait_send()

    @pl.when(me > 0)
    def _():
        z_send(0).wait_send()

    @pl.when(me < n_line - 1)
    def _():
        z_send(1).wait_send()

    to_solvers(lambda j: acd_copy(j).wait_send())
    to_solvers(lambda j: be_copy(j).wait_send())

    @pl.when(me < NV)
    def _():
        def done(d, c):
            ret_copy(lax.rem(me + d, n_line)).wait_send()
            return c

        lax.fori_loop(1, n_line, done, 0)

    for k in range(CH):
        residual_copy(k).wait()
        update_copy(k).wait()


def local(
    state, forcing, viscosity, coupling, thrust, disk_mask, block_inverse, lower_decay, upper_decay
):
    fields, depth, width, lanes = state.shape
    n_line = lax.axis_size("line")
    full = (fields, depth, width, lanes)
    f32 = jnp.float32
    V = pltpu.VMEM
    dma = pltpu.SemaphoreType.DMA
    hbm = pl.BlockSpec(memory_space=pltpu.HBM)
    return pl.pallas_call(
        kernel,
        out_shape=(pltpu.HBM(full, f32), pltpu.HBM(full, f32)),
        in_specs=[hbm] * 9,
        out_specs=(hbm, hbm),
        scratch_shapes=[
            V((fields, depth + 2, width, lanes), f32),
            V(full, f32),
            V((depth, width, lanes), jnp.int32),
            V((fields,) + full, f32),
            V(full, f32),
            V(full, f32),
            V(full, f32),
            V(full, f32),
            V(full, f32),
            V(full, f32),
            V(full, f32),
            V(full, f32),
            pltpu.SMEM((fields,), f32),
            pltpu.SMEM((fields, fields), f32),
            pltpu.SMEM((fields,), f32),
            V((2, fields, depth, lanes), f32),
            V((2, fields, depth, lanes), f32),
            V((NV, 3, 8, lanes), f32),
            V((n_line, 3, 8, lanes), f32),
            V((NV, 2, 8, lanes), f32),
            V((n_line, 2, 8, lanes), f32),
            V((n_line, 2, 8, lanes), f32),
            V((NV, 2, 8, lanes), f32),
            dma((3,)),
            dma((3,)),
            dma((3, CH)),
            dma((4,)),
            dma((4,)),
            dma((NV,)),
            dma,
            dma((NV,)),
            dma,
            dma((n_line,)),
            dma,
            dma((2, CH)),
        ],
        compiler_params=pltpu.CompilerParams(
            collective_id=0, has_side_effects=True, vmem_limit_bytes=48 * 1024 * 1024
        ),
    )(
        *(
            pltpu.with_memory_space_constraint(x, pltpu.HBM)
            for x in (
                viscosity, coupling, thrust, state, forcing, disk_mask, block_inverse, lower_decay, upper_decay
            )
        )
    )


def solution(mesh):
    in_specs = (
        P(None, "line", "blk", None),
        P(None, "line", "blk", None),
        P(),
        P(),
        P(),
        P("line", "blk", None),
        P(None, None, "line", "blk", None),
        P(None, "line", "blk", None),
        P(None, "line", "blk", None),
    )
    out_specs = (P(None, "line", "blk", None), P(None, "line", "blk", None))
    return jax.shard_map(local, mesh=mesh, in_specs=in_specs, out_specs=out_specs, check_vma=False)
```

```python
import jax
import jax.numpy as jnp
from jax import lax
from jax.experimental import pallas as pl
from jax.experimental.pallas import tpu as pltpu
from jax.sharding import PartitionSpec as P

F = 5
NV = 2 * F
CH = 4
UE = 2
UR = 2
US = 2
UB = 2
HALF = (slice(0, 8), slice(8, 16))


def planes(begin, count, unroll, body, carry, down=False):
    def some(i, carry):
        for j in range(unroll):
            z = i * unroll + j
            carry = body(begin - z if down else begin + z, carry)
        return carry

    return lax.fori_loop(0, count // unroll, some, carry)


def tiles(fn):
    return tuple(fn(c, h) for c in range(F) for h in range(2))


def segment_kernel(
    visc_h, coup_h, thr_h, state_h, forcing_h, mask_h, binv_h, lower_h, upper_h,
    u0, rr, vv, fo, ret,
    st, mk, bi, lo, up, gl, gu, qg, pp, sw,
    visc, coup, thr, xs, xh, zh, acd_s, acd_r, be_s, be_r, ret_s, ret_r,
    small_sem, load_sem, binv_sem, halo_ssem, halo_rsem,
    acd_ssem, acd_rsem, be_ssem, be_rsem, ret_ssem, ret_rsem,
):
    n_line = lax.axis_size("line")
    n_blk = lax.axis_size("blk")
    me = lax.axis_index("line")
    mb = lax.axis_index("blk")
    depth = lo.shape[1]
    step = depth // CH

    copy = pltpu.make_async_copy
    ld_state = copy(state_h, st.at[:, pl.ds(1, depth)], load_sem.at[0])
    ld_forcing = copy(forcing_h, fo, load_sem.at[1])
    ld_mask = copy(mask_h, mk, load_sem.at[2])
    ld_lower = copy(lower_h, lo, load_sem.at[3])
    ld_upper = copy(upper_h, up, load_sem.at[4])
    ld_small = [
        copy(src, dst, small_sem.at[i])
        for i, (src, dst) in enumerate(((visc_h, visc), (coup_h, coup), (thr_h, thr)))
    ]

    def ld_binv(k):
        part = pl.ds(k * step, step)
        return copy(binv_h.at[:, :, part], bi.at[:, :, part], binv_sem.at[k])

    ld_state.start()
    for cp in ld_small:
        cp.start()
    ld_forcing.start()
    ld_mask.start()
    ld_lower.start()
    ld_upper.start()

    def ahead(d):
        j = me + d
        return jnp.where(j >= n_line, j - n_line, j)

    barrier = pltpu.get_barrier_semaphore()
    for d in range(1, n_line):
        pl.semaphore_signal(barrier, inc=1, device_id={"line": ahead(d)})

    @pl.when(mb > 0)
    def _():
        pl.semaphore_signal(barrier, inc=1, device_id={"blk": mb - 1})

    @pl.when(mb < n_blk - 1)
    def _():
        pl.semaphore_signal(barrier, inc=1, device_id={"blk": mb + 1})

    for k in range(CH):
        ld_binv(k).start()

    zero_tile = jnp.zeros((8, 128), jnp.float32)
    one_tile = jnp.ones((8, 128), jnp.float32)
    for c in range(F):
        for sub in HALF:
            st[c, 0, sub, :] = zero_tile
            st[c, depth + 1, sub, :] = zero_tile

    ld_state.wait()
    for c in range(F):
        for side, row in ((0, 0), (1, 15)):
            xs[side, c] = st[c, 1 : depth + 1, row, :]

    beside_blk = jnp.where(mb > 0, 1, 0) + jnp.where(mb < n_blk - 1, 1, 0)
    pl.semaphore_wait(barrier, n_line - 1 + beside_blk)

    def z_send(side):
        return pltpu.make_async_remote_copy(
            src_ref=st.at[:, depth if side else 1], dst_ref=zh.at[1 - side],
            send_sem=halo_ssem.at[side], recv_sem=halo_rsem.at[side],
            device_id={"line": me + 1 if side else me - 1},
        )

    def x_send(side):
        return pltpu.make_async_remote_copy(
            src_ref=xs.at[side], dst_ref=xh.at[1 - side],
            send_sem=halo_ssem.at[2 + side], recv_sem=halo_rsem.at[2 + side],
            device_id={"blk": mb + 1 if side else mb - 1},
        )

    has_low, has_high = me > 0, me < n_line - 1
    has_left, has_right = mb > 0, mb < n_blk - 1
    halos = (
        (has_left, x_send(0), x_send(1)),
        (has_right, x_send(1), x_send(0)),
        (has_low, z_send(0), z_send(1)),
        (has_high, z_send(1), z_send(0)),
    )
    for cond, out, _ in halos:
        pl.when(cond)(out.start)

    ld_forcing.wait()
    ld_mask.wait()
    for cp in ld_small:
        cp.wait()
    rows = lax.broadcasted_iota(jnp.int32, (8, 128), 0)
    first = rows == 0
    last = rows == 7
    vis = [visc[c] for c in range(F)]
    mat = [[-coup[c, d] for d in range(F)] for c in range(F)]
    plain = [mat[c][c] - 6.0 * vis[c] for c in range(F)]
    sunk = [plain[c] - thr[c] for c in range(F)]

    def residual_plane(z, carry):
        cen = [[st[c, z + 1, sub, :] for sub in HALF] for c in range(F)]
        disk = [mk[z, sub, :] != 0 for sub in HALF]
        for c in range(F):
            v0, v1 = cen[c]
            r0, r1 = pltpu.roll(v0, 1, 0), pltpu.roll(v1, 1, 0)
            q0, q1 = pltpu.roll(v0, 7, 0), pltpu.roll(v1, 7, 0)
            xsum = (
                jnp.where(first, 0.0, r0) + jnp.where(last, q1, q0),
                jnp.where(first, r0, r1) + jnp.where(last, 0.0, q1),
            )
            for h, sub in enumerate(HALF):
                v = cen[c][h]
                beside = (st[c, z, sub, :] + st[c, z + 2, sub, :]) + xsum[h]
                beside = beside + (pltpu.roll(v, 1, 1) + pltpu.roll(v, 127, 1))
                total = fo[c, z, sub, :] + vis[c] * beside
                total = total + jnp.where(disk[h], sunk[c], plain[c]) * v
                for d in range(F):
                    if d != c:
                        total = total + mat[c][d] * cen[d][h]
                fo[c, z, sub, :] = total
        return carry

    planes(0, depth, UR, residual_plane, 0)

    ld_lower.wait()
    ld_upper.wait()

    def decay_plane(z, carry):
        new = []
        for i, (p, q, r) in enumerate(carry):
            c, sub = i // 2, HALF[i % 2]
            l, u = lo[c, z, sub, :], up[c, z, sub, :]
            l2 = 1.0 - l * l
            u2 = 1.0 - u * u
            g = u2 * lax.rsqrt(u2)
            gl[c, z, sub, :] = l2 * lax.rsqrt(l2)
            gu[c, z, sub, :] = g
            p = p * l
            w = q * g
            pp[c, z, sub, :] = p
            qg[c, z, sub, :] = w
            new.append((p, q * u, r + w * p))
        return tuple(new)

    acd = planes(0, depth, UE, decay_plane, ((one_tile, one_tile, zero_tile),) * NV)
    for v in range(NV):
        for i in range(3):
            acd_s[v, i] = acd[v][i]

    def to_solvers(src, dst, ssem, rsem):
        for d in range(1, n_line):
            j = ahead(d)

            @pl.when(j < NV)
            def _():
                pltpu.make_async_remote_copy(
                    src_ref=src.at[j], dst_ref=dst.at[me], send_sem=ssem, recv_sem=rsem,
                    device_id={"line": j},
                ).start()

    def drain(ref, sem):
        copy(ref, ref, sem).wait()

    to_solvers(acd_s, acd_r, acd_ssem, acd_rsem)

    pl.when(has_left)(halos[0][2].wait_recv)
    pl.when(has_right)(halos[1][2].wait_recv)
    pl.when(has_low)(halos[2][2].wait_recv)
    pl.when(has_high)(halos[3][2].wait_recv)

    def add_x(side, row):
        for c in range(F):
            fo[c, :, row, :] = fo[c, :, row, :] + vis[c] * xh[side, c]

    def add_z(side, z):
        for c in range(F):
            fo[c, z] = fo[c, z] + vis[c] * zh[side, c]

    pl.when(has_left)(lambda: add_x(0, 0))
    pl.when(has_right)(lambda: add_x(1, 15))
    pl.when(has_low)(lambda: add_z(0, 0))
    pl.when(has_high)(lambda: add_z(1, depth - 1))

    def sweep_plane(z, carry):
        s, e = carry
        new_s, new_e = [], []
        for i in range(NV):
            c, sub = i // 2, HALF[i % 2]
            src = bi[c, 0, z, sub, :] * fo[0, z, sub, :]
            for d in range(1, F):
                src = src + bi[c, d, z, sub, :] * fo[d, z, sub, :]
            v = lo[c, z, sub, :] * s[i] + gl[c, z, sub, :] * src
            sw[c, z, sub, :] = v
            new_s.append(v)
            new_e.append(e[i] + qg[c, z, sub, :] * v)
        return tuple(new_s), tuple(new_e)

    carry = ((zero_tile,) * NV, (zero_tile,) * NV)

    def sweep_chunk(k, carry):
        ld_binv(k).wait()
        return planes(k * step, step, US, sweep_plane, carry)

    b_all, e_all = lax.fori_loop(0, CH, sweep_chunk, carry)
    for v in range(NV):
        be_s[v, 0] = b_all[v]
        be_s[v, 1] = e_all[v]
    to_solvers(be_s, be_r, be_ssem, be_rsem)

    def down_plane(z, carry):
        new = []
        for i, (u, r, v) in enumerate(carry):
            c, sub = i // 2, HALF[i % 2]
            a, g = up[c, z, sub, :], gu[c, z, sub, :]
            u = a * u + g * sw[c, z, sub, :]
            r = a * r + g * pp[c, z, sub, :]
            v = a * v
            u0[c, z, sub, :] = u
            rr[c, z, sub, :] = r
            vv[c, z, sub, :] = v
            new.append((u, r, v))
        return tuple(new)

    planes(depth - 1, depth, UB, down_plane, ((zero_tile, zero_tile, one_tile),) * NV, down=True)

    @pl.when(me < NV)
    def _():
        acd_r[me] = acd_s[me]
        be_r[me] = be_s[me]
        drain(acd_r.at[pl.ds(0, n_line - 1)], acd_rsem)
        drain(be_r.at[pl.ds(0, n_line - 1)], be_rsem)
        s = zero_tile
        t = []
        for k in range(n_line):
            ret_s[k, 0] = s
            t.append(acd_r[k, 2] * s + be_r[k, 1])
            s = acd_r[k, 0] * s + be_r[k, 0]
        u = zero_tile
        for k in range(n_line - 1, -1, -1):
            ret_s[k, 1] = u
            u = acd_r[k, 1] * u + t[k]
        for d in range(1, n_line):
            k = ahead(d)
            pltpu.make_async_remote_copy(
                src_ref=ret_s.at[k], dst_ref=ret_r.at[me], send_sem=ret_ssem, recv_sem=ret_rsem,
                device_id={"line": k},
            ).start()
        ret_r[me] = ret_s[me]
        drain(acd_s.at[pl.ds(0, NV - 1)], acd_ssem)
        drain(be_s.at[pl.ds(0, NV - 1)], be_ssem)
        drain(ret_s.at[pl.ds(0, n_line - 1)], ret_ssem)
        drain(ret_r.at[pl.ds(0, NV - 1)], ret_rsem)

    @pl.when(me >= NV)
    def _():
        drain(acd_s, acd_ssem)
        drain(be_s, be_ssem)
        drain(ret_r, ret_rsem)

    for v in range(NV):
        for i in range(2):
            ret[v, i] = ret_r[v, i]

    for cond, out, _ in halos:
        pl.when(cond)(out.wait_send)


def finish_kernel(u0, rr, vv, fo, ret, update_h, resid_h, out, res_sem, out_sem):
    depth = u0.shape[1]
    step = depth // CH
    write_res = pltpu.make_async_copy(fo, resid_h, res_sem)
    write_res.start()

    def update_copy(k):
        part = pl.ds(k * step, step)
        return pltpu.make_async_copy(out.at[:, part], update_h.at[:, part], out_sem.at[k])

    s_in = tiles(lambda c, h: ret[2 * c + h, 0])
    u_in = tiles(lambda c, h: ret[2 * c + h, 1])

    def plane(z, carry):
        for i in range(NV):
            c, sub = i // 2, HALF[i % 2]
            out[c, z, sub, :] = u0[c, z, sub, :] + rr[c, z, sub, :] * s_in[i] + vv[c, z, sub, :] * u_in[i]
        return carry

    for k in range(CH):
        planes(k * step, step, 2, plane, 0)
        update_copy(k).start()
    write_res.wait()
    for k in range(CH):
        update_copy(k).wait()


def local(
    state, forcing, viscosity, coupling, thrust, disk_mask, block_inverse, lower_decay, upper_decay
):
    fields, depth, width, lanes = state.shape
    n_line = lax.axis_size("line")
    full = (fields, depth, width, lanes)
    f32 = jnp.float32
    V = pltpu.VMEM
    dma = pltpu.SemaphoreType.DMA
    hbm = pl.BlockSpec(memory_space=pltpu.HBM)
    vmem = pl.BlockSpec(memory_space=pltpu.VMEM)
    args = (viscosity, coupling, thrust, state, forcing, disk_mask, block_inverse, lower_decay, upper_decay)
    parts = pl.pallas_call(
        segment_kernel,
        out_shape=(V(full, f32),) * 4 + (V((NV, 2, 8, lanes), f32),),
        in_specs=[hbm] * len(args),
        out_specs=(vmem,) * 5,
        scratch_shapes=[
            V((fields, depth + 2, width, lanes), f32),
            V((depth, width, lanes), jnp.int32),
            V((fields,) + full, f32),
            V(full, f32),
            V(full, f32),
            V(full, f32),
            V(full, f32),
            V(full, f32),
            V(full, f32),
            V(full, f32),
            pltpu.SMEM((fields,), f32),
            pltpu.SMEM((fields, fields), f32),
            pltpu.SMEM((fields,), f32),
            V((2, fields, depth, lanes), f32),
            V((2, fields, depth, lanes), f32),
            V((2, fields, width, lanes), f32),
            V((NV, 3, 8, lanes), f32),
            V((n_line, 3, 8, lanes), f32),
            V((NV, 2, 8, lanes), f32),
            V((n_line, 2, 8, lanes), f32),
            V((n_line, 2, 8, lanes), f32),
            V((NV, 2, 8, lanes), f32),
            dma((3,)),
            dma((5,)),
            dma((CH,)),
            dma((4,)),
            dma((4,)),
            dma, dma, dma, dma, dma, dma,
        ],
        compiler_params=pltpu.CompilerParams(
            collective_id=0, has_side_effects=True, vmem_limit_bytes=40 * 1024 * 1024
        ),
    )(*(pltpu.with_memory_space_constraint(x, pltpu.HBM) for x in args))
    return pl.pallas_call(
        finish_kernel,
        out_shape=(pltpu.HBM(full, f32), pltpu.HBM(full, f32)),
        in_specs=[vmem] * 5,
        out_specs=(hbm, hbm),
        scratch_shapes=[V(full, f32), dma, dma((CH,))],
        compiler_params=pltpu.CompilerParams(vmem_limit_bytes=16 * 1024 * 1024),
    )(*(pltpu.with_memory_space_constraint(x, pltpu.VMEM) for x in parts))


def solution(mesh):
    in_specs = (
        P(None, "line", "blk", None),
        P(None, "line", "blk", None),
        P(),
        P(),
        P(),
        P("line", "blk", None),
        P(None, None, "line", "blk", None),
        P(None, "line", "blk", None),
        P(None, "line", "blk", None),
    )
    out_specs = (P(None, "line", "blk", None), P(None, "line", "blk", None))
    return jax.shard_map(local, mesh=mesh, in_specs=in_specs, out_specs=out_specs, check_vma=False)
```

```python
import jax
import jax.numpy as jnp
from jax import lax
from jax.experimental import pallas as pl
from jax.experimental.pallas import tpu as pltpu
from jax.sharding import PartitionSpec as P

F = 5
NV = 2 * F
CH = 4
UE = 2
UR = 2
US = 2
UB = 2
HALF = (slice(0, 8), slice(8, 16))
NXC = NYC = 4
SOLVERS = (
    ((0, 1), (3, 1), (12, 1), (15, 1), (4, 1), (8, 1), (7, 1), (11, 1), (13, 1), (1, 1)),
    ((5, 1), (6, 1), (9, 1), (10, 1), (2, 1), (14, 1), (4, 0), (8, 0), (7, 0), (1, 0)),
)
ORDER = (0, 1, 4, 3, 12, 2, 8, 5, 13, 7, 6, 9, 15, 14, 11, 10)


def planes(begin, count, unroll, body, carry, down=False):
    def one(z, carry):
        return body(begin - z if down else begin + z, carry)

    def some(i, carry):
        for j in range(unroll):
            carry = one(i * unroll + j, carry)
        return carry

    carry = lax.fori_loop(0, count // unroll, some, carry)
    for z in range(count - count % unroll, count):
        carry = one(z, carry)
    return carry


def tiles(fn):
    return tuple(fn(c, h) for c in range(F) for h in range(2))


def segment_kernel(
    visc_h, coup_h, thr_h, state_h, forcing_h, mask_h, binv_h, lower_h, upper_h,
    u0, rr, vv, fo, ret,
    st, mk, bi, lo, up, gl, gu, qg, pp, sw,
    visc, coup, thr, xs, xh, zh, low, acd_s, acd_r, be_s, be_r, ret_s, ret_r,
    small_sem, load_sem, binv_sem, halo_ssem, halo_rsem,
    acd_ssem, acd_rsem, be_ssem, be_rsem, ret_ssem, ret_rsem, row_sem, pair_sem,
):
    n_line = lax.axis_size("line")
    n_blk = lax.axis_size("blk")
    me = lax.axis_index("line")
    mb = lax.axis_index("blk")
    x, y, core = me // NYC, me % NYC, mb % 2
    depth = lo.shape[1]
    step = depth // CH
    half = depth // 2

    copy = pltpu.make_async_copy
    ld_state = copy(state_h, st.at[:, pl.ds(1, depth)], load_sem.at[0])
    ld_forcing = copy(forcing_h, fo, load_sem.at[1])
    ld_mask = copy(mask_h, mk, load_sem.at[2])
    ld_lower = copy(lower_h, lo, load_sem.at[3])
    ld_upper = copy(upper_h, up, load_sem.at[4])
    ld_small = [
        copy(src, dst, small_sem.at[i])
        for i, (src, dst) in enumerate(((visc_h, visc), (coup_h, coup), (thr_h, thr)))
    ]

    def ld_binv(k):
        part = pl.ds(k * step, step)
        return copy(binv_h.at[:, :, part], bi.at[:, :, part], binv_sem.at[k])

    ld_state.start()
    for cp in ld_small:
        cp.start()
    ld_forcing.start()
    ld_mask.start()
    ld_lower.start()
    ld_upper.start()

    has_low, has_high = me > 0, me < n_line - 1
    has_left, has_right = mb > 0, mb < n_blk - 1
    turn_low = jnp.logical_and(has_low, y == 0)
    turn_high = jnp.logical_and(has_high, y == NYC - 1)
    barrier = pltpu.get_barrier_semaphore()

    def greet(**device):
        pl.semaphore_signal(barrier, inc=1, device_id=device)

    def wrap(v, n):
        return jnp.where(v >= n, v - n, v)

    def in_column(d):
        return wrap(x + d, NXC) * NYC + y

    pl.when(has_left)(lambda: greet(blk=mb - 1))
    pl.when(has_right)(lambda: greet(blk=mb + 1))
    pl.when(turn_low)(lambda: greet(line=me - 1))
    pl.when(turn_high)(lambda: greet(line=me + 1))
    for d in range(1, NYC):
        greet(line=x * NYC + wrap(y + d, NYC))
    for d in range(1, NXC):
        greet(line=in_column(d))

    for k in range(CH):
        ld_binv(k).start()

    zero_tile = jnp.zeros((8, 128), jnp.float32)
    one_tile = jnp.ones((8, 128), jnp.float32)
    for c in range(F):
        for sub in HALF:
            st[c, 0, sub, :] = zero_tile
            st[c, depth + 1, sub, :] = zero_tile
            sw[c, 0, sub, :] = zero_tile

    ld_state.wait()
    for c in range(F):
        for side, row in ((0, 0), (1, 15)):
            xs[side, c] = st[c, 1 : depth + 1, row, :]

    greeted = NYC - 1 + NXC - 1
    for cond in (has_left, has_right, turn_low, turn_high):
        greeted = greeted + jnp.where(cond, 1, 0)
    pl.semaphore_wait(barrier, greeted)

    def z_send(side):
        return pltpu.make_async_remote_copy(
            src_ref=st.at[:, depth if side else 1], dst_ref=zh.at[1 - side],
            send_sem=halo_ssem.at[side], recv_sem=halo_rsem.at[side],
            device_id={"line": me + 1 if side else me - 1},
        )

    def x_send(side, part):
        zs = pl.ds(part * half, half)
        return pltpu.make_async_remote_copy(
            src_ref=xs.at[side, :, zs], dst_ref=xh.at[1 - side, :, zs],
            send_sem=halo_ssem.at[2 + 2 * part + side], recv_sem=halo_rsem.at[2 + 2 * part + side],
            device_id={"blk": mb + 1 if side else mb - 1},
        )

    outgoing = (
        (has_low, z_send(0)),
        (has_high, z_send(1)),
        (has_left, x_send(0, 0)),
        (has_right, x_send(1, 0)),
        (has_left, x_send(0, 1)),
        (has_right, x_send(1, 1)),
    )
    for cond, out in outgoing:
        pl.when(cond)(out.start)

    for d in range(1, NXC):
        pl.semaphore_signal(row_sem, inc=1, device_id={"line": in_column(d)})

    ld_forcing.wait()
    ld_mask.wait()
    for cp in ld_small:
        cp.wait()
    rows = lax.broadcasted_iota(jnp.int32, (8, 128), 0)
    first = rows == 0
    last = rows == 7
    vis = [visc[c] for c in range(F)]
    mat = [[-coup[c, d] for d in range(F)] for c in range(F)]
    plain = [mat[c][c] - 6.0 * vis[c] for c in range(F)]
    sunk = [plain[c] - thr[c] for c in range(F)]

    def residual_plane(z, carry):
        cen = [[st[c, z + 1, sub, :] for sub in HALF] for c in range(F)]
        disk = [mk[z, sub, :] != 0 for sub in HALF]
        for c in range(F):
            v0, v1 = cen[c]
            r0, r1 = pltpu.roll(v0, 1, 0), pltpu.roll(v1, 1, 0)
            q0, q1 = pltpu.roll(v0, 7, 0), pltpu.roll(v1, 7, 0)
            xsum = (
                jnp.where(first, 0.0, r0) + jnp.where(last, q1, q0),
                jnp.where(first, r0, r1) + jnp.where(last, 0.0, q1),
            )
            for h, sub in enumerate(HALF):
                v = cen[c][h]
                beside = (st[c, z, sub, :] + st[c, z + 2, sub, :]) + xsum[h]
                beside = beside + (pltpu.roll(v, 1, 1) + pltpu.roll(v, 127, 1))
                total = fo[c, z, sub, :] + vis[c] * beside
                total = total + jnp.where(disk[h], sunk[c], plain[c]) * v
                for d in range(F):
                    if d != c:
                        total = total + mat[c][d] * cen[d][h]
                fo[c, z, sub, :] = total
        return carry

    planes(0, depth, UR, residual_plane, 0)

    ld_lower.wait()
    ld_upper.wait()
    for c in range(F):
        for h, sub in enumerate(HALF):
            low[c, h] = lo[c, 0, sub, :]
            lo[c, 0, sub, :] = one_tile


    def decay_plane(z, carry):
        new = []
        for i, (p, q, r) in enumerate(carry):
            c, sub = i // 2, HALF[i % 2]
            l, u = lo[c, z, sub, :], up[c, z, sub, :]
            l2 = 1.0 - l * l
            u2 = 1.0 - u * u
            g = u2 * lax.rsqrt(u2)
            gl[c, z, sub, :] = l2 * lax.rsqrt(l2)
            gu[c, z, sub, :] = g
            p = p * l
            w = q * g
            pp[c, z, sub, :] = p
            qg[c, z, sub, :] = w
            new.append((p, q * u, r + w * p))
        return tuple(new)

    acd = planes(0, depth, UE, decay_plane, ((one_tile, one_tile, zero_tile),) * NV)
    for c in range(F):
        for h, sub in enumerate(HALF):
            l2 = 1.0 - low[c, h] * low[c, h]
            gl[c, 0, sub, :] = l2 * lax.rsqrt(l2)
            p, q, r = acd[2 * c + h]
            acd_s[2 * c + h, 0] = p * low[c, h]
            acd_s[2 * c + h, 1] = q
            acd_s[2 * c + h, 2] = r * low[c, h]

    pl.semaphore_wait(row_sem, NXC - 1)

    other = mb + 1 - 2 * core
    pl.semaphore_signal(pair_sem, inc=1, device_id={"blk": other})
    pl.semaphore_wait(pair_sem, 1)

    def drain(ref, sem):
        copy(ref, ref, sem).wait()

    def to_solvers(src, dst, ssem, rsem):
        for mine in range(2):

            @pl.when(core == mine)
            def _():
                for v, (line, at) in enumerate(SOLVERS[mine]):
                    out = pltpu.make_async_remote_copy(
                        src_ref=src.at[v], dst_ref=dst.at[me], send_sem=ssem, recv_sem=rsem,
                        device_id={"line": line, "blk": mb if at == mine else other},
                    )
                    if at == mine:
                        pl.when(me != line)(out.start)
                    else:
                        out.start()

    to_solvers(acd_s, acd_r, acd_ssem, acd_rsem)

    def source(z, i):
        c, sub = i // 2, HALF[i % 2]
        src = bi[c, 0, z, sub, :] * fo[0, z, sub, :]
        for d in range(1, F):
            src = src + bi[c, d, z, sub, :] * fo[d, z, sub, :]
        return gl[c, z, sub, :] * src

    def sweep_plane(z, carry):
        s, e = carry
        new_s, new_e = [], []
        for i in range(NV):
            c, sub = i // 2, HALF[i % 2]
            v = lo[c, z, sub, :] * s[i] + source(z, i)
            sw[c, z, sub, :] = v
            new_s.append(v)
            new_e.append(e[i] + qg[c, z, sub, :] * v)
        return tuple(new_s), tuple(new_e)

    def add_x(side, part, row):
        zs = slice(part * half, part * half + half)
        for c in range(F):
            fo[c, zs, row, :] = fo[c, zs, row, :] + vis[c] * xh[side, c, zs]

    def add_z(side, z):
        for c in range(F):
            fo[c, z] = fo[c, z] + vis[c] * zh[side, c]

    def x_halo(part):
        @pl.when(has_left)
        def _():
            x_send(1, part).wait_recv()
            add_x(0, part, 0)

        @pl.when(has_right)
        def _():
            x_send(0, part).wait_recv()
            add_x(1, part, 15)

    carry = ((zero_tile,) * NV, (zero_tile,) * NV)
    for k in range(CH):
        if k * step % half == 0:
            x_halo(k * step // half)
        ld_binv(k).wait()
        begin = max(k * step, 1)
        end = min((k + 1) * step, depth - 1)
        carry = planes(begin, end - begin, US, sweep_plane, carry)

    @pl.when(has_high)
    def _():
        z_send(0).wait_recv()
        add_z(1, depth - 1)

    s_all, e_all = sweep_plane(depth - 1, carry)

    @pl.when(has_low)
    def _():
        z_send(1).wait_recv()
        add_z(0, 0)

    for i in range(NV):
        c, h = i // 2, i % 2
        p, q, r = acd[i]
        s0 = source(0, i)
        be_s[i, 0] = s_all[i] + p * s0
        be_s[i, 1] = e_all[i] + r * s0
        ret[c, h, 0] = s0
    to_solvers(be_s, be_r, be_ssem, be_rsem)

    def down_plane(z, carry):
        new = []
        for i, (u, r, v) in enumerate(carry):
            c, sub = i // 2, HALF[i % 2]
            a, g = up[c, z, sub, :], gu[c, z, sub, :]
            u = a * u + g * sw[c, z, sub, :]
            r = a * r + g * pp[c, z, sub, :]
            v = a * v
            u0[c, z, sub, :] = u
            rr[c, z, sub, :] = r
            vv[c, z, sub, :] = v
            new.append((u, r, v))
        return tuple(new)

    planes(depth - 1, depth, UB, down_plane, ((zero_tile, zero_tile, one_tile),) * NV, down=True)

    def role(cross):
        found, tile = False, 0
        for mine in range(2):
            for v, (line, at) in enumerate(SOLVERS[mine]):
                if (at != mine) == cross:
                    here = jnp.logical_and(core == at, me == line)
                    found = jnp.logical_or(found, here)
                    tile = jnp.where(here, v, tile)
        return found, tile

    def solve(tile, cross):
        count = n_line if cross else n_line - 1
        if not cross:
            acd_r[me] = acd_s[tile]
            be_r[me] = be_s[tile]
        drain(acd_r.at[pl.ds(0, count)], acd_rsem)
        drain(be_r.at[pl.ds(0, count)], be_rsem)
        s = zero_tile
        t = []
        for k in range(n_line):
            ret_s[k, 0] = s
            t.append(acd_r[k, 2] * s + be_r[k, 1])
            s = acd_r[k, 0] * s + be_r[k, 0]
        u = zero_tile
        for k in range(n_line - 1, -1, -1):
            ret_s[k, 1] = u
            u = acd_r[k, 1] * u + t[k]
        for k in ORDER:
            out = pltpu.make_async_remote_copy(
                src_ref=ret_s.at[k], dst_ref=ret_r.at[tile], send_sem=ret_ssem, recv_sem=ret_rsem,
                device_id={"line": k, "blk": other if cross else mb},
            )
            if cross:
                out.start()
            else:
                pl.when(me != k)(out.start)
        if not cross:
            ret_r[tile] = ret_s[me]

    solves_other, other_tile = role(True)
    solves_own, own_tile = role(False)

    @pl.when(solves_other)
    def _():
        solve(other_tile, True)
        drain(ret_s, ret_ssem)

    @pl.when(solves_own)
    def _():
        solve(own_tile, False)
        drain(ret_r.at[pl.ds(0, NV - 1)], ret_rsem)
        drain(ret_s.at[pl.ds(0, n_line - 1)], ret_ssem)
        drain(acd_s.at[pl.ds(0, NV - 1)], acd_ssem)
        drain(be_s.at[pl.ds(0, NV - 1)], be_ssem)

    @pl.when(jnp.logical_not(solves_own))
    def _():
        drain(ret_r, ret_rsem)
        drain(acd_s, acd_ssem)
        drain(be_s, be_ssem)

    for c in range(F):
        for h in range(2):
            ret[c, h, 0] = ret[c, h, 0] + low[c, h] * ret_r[2 * c + h, 0]
            ret[c, h, 1] = ret_r[2 * c + h, 1]

    for cond, out in outgoing:
        pl.when(cond)(out.wait_send)


def finish_kernel(u0, rr, vv, fo, ret, update_h, resid_h, out, res_sem, out_sem):
    depth = u0.shape[1]
    step = depth // CH
    write_res = pltpu.make_async_copy(fo, resid_h, res_sem)
    write_res.start()

    def update_copy(k):
        part = pl.ds(k * step, step)
        return pltpu.make_async_copy(out.at[:, part], update_h.at[:, part], out_sem.at[k])

    s_in = tiles(lambda c, h: ret[c, h, 0])
    u_in = tiles(lambda c, h: ret[c, h, 1])

    def plane(z, carry):
        for i in range(NV):
            c, sub = i // 2, HALF[i % 2]
            out[c, z, sub, :] = u0[c, z, sub, :] + rr[c, z, sub, :] * s_in[i] + vv[c, z, sub, :] * u_in[i]
        return carry

    for k in range(CH):
        planes(k * step, step, 2, plane, 0)
        update_copy(k).start()
    write_res.wait()
    for k in range(CH):
        update_copy(k).wait()


def local(
    state, forcing, viscosity, coupling, thrust, disk_mask, block_inverse, lower_decay, upper_decay
):
    fields, depth, width, lanes = state.shape
    n_line = lax.axis_size("line")
    full = (fields, depth, width, lanes)
    f32 = jnp.float32
    V = pltpu.VMEM
    dma = pltpu.SemaphoreType.DMA
    hbm = pl.BlockSpec(memory_space=pltpu.HBM)
    vmem = pl.BlockSpec(memory_space=pltpu.VMEM)
    args = (viscosity, coupling, thrust, state, forcing, disk_mask, block_inverse, lower_decay, upper_decay)
    parts = pl.pallas_call(
        segment_kernel,
        out_shape=(V(full, f32),) * 4 + (V((fields, 2, 2, 8, lanes), f32),),
        in_specs=[hbm] * len(args),
        out_specs=(vmem,) * 5,
        scratch_shapes=[
            V((fields, depth + 2, width, lanes), f32),
            V((depth, width, lanes), jnp.int32),
            V((fields,) + full, f32),
            V(full, f32),
            V(full, f32),
            V(full, f32),
            V(full, f32),
            V(full, f32),
            V(full, f32),
            V(full, f32),
            pltpu.SMEM((fields,), f32),
            pltpu.SMEM((fields, fields), f32),
            pltpu.SMEM((fields,), f32),
            V((2, fields, depth, lanes), f32),
            V((2, fields, depth, lanes), f32),
            V((2, fields, width, lanes), f32),
            V((fields, 2, 8, lanes), f32),
            V((NV, 3, 8, lanes), f32),
            V((n_line, 3, 8, lanes), f32),
            V((NV, 2, 8, lanes), f32),
            V((n_line, 2, 8, lanes), f32),
            V((n_line, 2, 8, lanes), f32),
            V((NV, 2, 8, lanes), f32),
            dma((3,)),
            dma((5,)),
            dma((CH,)),
            dma((6,)),
            dma((6,)),
            dma, dma, dma, dma, dma, dma,
            pltpu.SemaphoreType.REGULAR,
            pltpu.SemaphoreType.REGULAR,
        ],
        compiler_params=pltpu.CompilerParams(
            collective_id=0, has_side_effects=True, vmem_limit_bytes=40 * 1024 * 1024
        ),
    )(*(pltpu.with_memory_space_constraint(x, pltpu.HBM) for x in args))
    return pl.pallas_call(
        finish_kernel,
        out_shape=(pltpu.HBM(full, f32), pltpu.HBM(full, f32)),
        in_specs=[vmem] * 5,
        out_specs=(hbm, hbm),
        scratch_shapes=[V(full, f32), dma, dma((CH,))],
        compiler_params=pltpu.CompilerParams(vmem_limit_bytes=16 * 1024 * 1024),
    )(*(pltpu.with_memory_space_constraint(x, pltpu.VMEM) for x in parts))


def solution(mesh):
    in_specs = (
        P(None, "line", "blk", None),
        P(None, "line", "blk", None),
        P(),
        P(),
        P(),
        P("line", "blk", None),
        P(None, None, "line", "blk", None),
        P(None, "line", "blk", None),
        P(None, "line", "blk", None),
    )
    out_specs = (P(None, "line", "blk", None), P(None, "line", "blk", None))
    return jax.shard_map(local, mesh=mesh, in_specs=in_specs, out_specs=out_specs, check_vma=False)
```

```python
import jax
import jax.numpy as jnp
from jax import lax
from jax.experimental import pallas as pl
from jax.experimental.pallas import tpu as pltpu
from jax.sharding import PartitionSpec as P

F = 5
NV = 2 * F
CH = 4
XP = 1
UE = 4
UR = 8
US = 4
UB = 4
UF = 2
CF = 4
HALF = (slice(0, 8), slice(8, 16))
NXC = NYC = 4
SOLVERS = (
    ((0, 0), (3, 0), (4, 0), (12, 0), (9, 1), (5, 1), (13, 1), (6, 1), (10, 1), (14, 1)),
    ((0, 1), (4, 1), (12, 1), (15, 1), (3, 1), (8, 1), (1, 1), (2, 1), (11, 1), (7, 1)),
)
ORDER = (0, 1, 4, 3, 12, 2, 8, 5, 13, 7, 6, 9, 15, 14, 11, 10)


def planes(begin, count, unroll, body, carry, down=False):
    def one(z, carry):
        return body(begin - z if down else begin + z, carry)

    def some(i, carry):
        for j in range(unroll):
            carry = one(i * unroll + j, carry)
        return carry

    carry = lax.fori_loop(0, count // unroll, some, carry)
    for z in range(count - count % unroll, count):
        carry = one(z, carry)
    return carry


def tiles(fn):
    return tuple(fn(c, h) for c in range(F) for h in range(2))


def segment_kernel(
    visc_h, coup_h, thr_h, state_h, forcing_h, mask_h, binv_h, lower_h, upper_h,
    u0, rr, vv, fo, ret,
    st, mk, bi, lo, up, gl, gu, qg, pp, sw,
    visc, coup, thr, xs, xh, zh, low, acd_s, acd_r, be_s, be_r, ret_s, ret_r,
    small_sem, load_sem, binv_sem, halo_ssem, halo_rsem,
    acd_ssem, acd_rsem, be_ssem, be_rsem, ret_ssem, ret_rsem, row_sem, pair_sem,
):
    n_line = lax.axis_size("line")
    n_blk = lax.axis_size("blk")
    me = lax.axis_index("line")
    mb = lax.axis_index("blk")
    x, y, core = me // NYC, me % NYC, mb % 2
    depth = lo.shape[1]
    step = depth // CH
    piece = depth // XP

    copy = pltpu.make_async_copy
    ld_state = copy(state_h, st.at[:, pl.ds(1, depth)], load_sem.at[0])
    ld_forcing = copy(forcing_h, fo, load_sem.at[1])
    ld_mask = copy(mask_h, mk, load_sem.at[2])
    ld_lower = copy(lower_h, lo, load_sem.at[3])
    ld_upper = copy(upper_h, up, load_sem.at[4])
    ld_small = [
        copy(src, dst, small_sem.at[i])
        for i, (src, dst) in enumerate(((visc_h, visc), (coup_h, coup), (thr_h, thr)))
    ]

    def ld_binv(k):
        part = pl.ds(k * step, step)
        return copy(binv_h.at[:, :, part], bi.at[:, :, part], binv_sem.at[k])

    ld_state.start()
    for cp in ld_small:
        cp.start()
    ld_forcing.start()
    ld_mask.start()
    ld_lower.start()
    ld_upper.start()

    has_low, has_high = me > 0, me < n_line - 1
    has_left, has_right = mb > 0, mb < n_blk - 1
    turn_low = jnp.logical_and(has_low, y == 0)
    turn_high = jnp.logical_and(has_high, y == NYC - 1)
    barrier = pltpu.get_barrier_semaphore()

    def greet(**device):
        pl.semaphore_signal(barrier, inc=1, device_id=device)

    def wrap(v, n):
        return jnp.where(v >= n, v - n, v)

    def in_column(d):
        return wrap(x + d, NXC) * NYC + y

    pl.when(has_left)(lambda: greet(blk=mb - 1))
    pl.when(has_right)(lambda: greet(blk=mb + 1))
    pl.when(turn_low)(lambda: greet(line=me - 1))
    pl.when(turn_high)(lambda: greet(line=me + 1))
    for d in range(1, NYC):
        greet(line=x * NYC + wrap(y + d, NYC))
    for d in range(1, NXC):
        greet(line=in_column(d))

    for k in range(CH):
        ld_binv(k).start()

    zero_tile = jnp.zeros((8, 128), jnp.float32)
    one_tile = jnp.ones((8, 128), jnp.float32)
    for c in range(F):
        for sub in HALF:
            st[c, 0, sub, :] = zero_tile
            st[c, depth + 1, sub, :] = zero_tile
            sw[c, 0, sub, :] = zero_tile

    ld_state.wait()
    for c in range(F):
        for side, row in ((0, 0), (1, 15)):
            xs[side, c] = st[c, 1 : depth + 1, row, :]

    greeted = NYC - 1 + NXC - 1
    for cond in (has_left, has_right, turn_low, turn_high):
        greeted = greeted + jnp.where(cond, 1, 0)
    pl.semaphore_wait(barrier, greeted)

    def z_send(side):
        return pltpu.make_async_remote_copy(
            src_ref=st.at[:, depth if side else 1], dst_ref=zh.at[1 - side],
            send_sem=halo_ssem.at[side], recv_sem=halo_rsem.at[side],
            device_id={"line": me + 1 if side else me - 1},
        )

    def x_send(side, part):
        zs = pl.ds(part * piece, piece)
        return pltpu.make_async_remote_copy(
            src_ref=xs.at[side, :, zs], dst_ref=xh.at[1 - side, :, zs],
            send_sem=halo_ssem.at[2 + 2 * part + side], recv_sem=halo_rsem.at[2 + 2 * part + side],
            device_id={"blk": mb + 1 if side else mb - 1},
        )

    outgoing = (
        (has_low, z_send(0)),
        (has_high, z_send(1)),
    ) + tuple(
        (cond, x_send(side, part)) for part in range(XP) for side, cond in ((0, has_left), (1, has_right))
    )
    for cond, out in outgoing:
        pl.when(cond)(out.start)

    for d in range(1, NXC):
        pl.semaphore_signal(row_sem, inc=1, device_id={"line": in_column(d)})

    ld_forcing.wait()
    ld_mask.wait()
    for cp in ld_small:
        cp.wait()
    rows = lax.broadcasted_iota(jnp.int32, (8, 128), 0)
    first = rows == 0
    last = rows == 7
    vis = [visc[c] for c in range(F)]
    mat = [[-coup[c, d] for d in range(F)] for c in range(F)]
    plain = [mat[c][c] - 6.0 * vis[c] for c in range(F)]
    sunk = [plain[c] - thr[c] for c in range(F)]

    def residual_plane(z, carry):
        cen = [[st[c, z + 1, sub, :] for sub in HALF] for c in range(F)]
        disk = [mk[z, sub, :] != 0 for sub in HALF]
        for c in range(F):
            v0, v1 = cen[c]
            r0, r1 = pltpu.roll(v0, 1, 0), pltpu.roll(v1, 1, 0)
            q0, q1 = pltpu.roll(v0, 7, 0), pltpu.roll(v1, 7, 0)
            xsum = (
                jnp.where(first, 0.0, r0) + jnp.where(last, q1, q0),
                jnp.where(first, r0, r1) + jnp.where(last, 0.0, q1),
            )
            for h, sub in enumerate(HALF):
                v = cen[c][h]
                beside = (st[c, z, sub, :] + st[c, z + 2, sub, :]) + xsum[h]
                beside = beside + (pltpu.roll(v, 1, 1) + pltpu.roll(v, 127, 1))
                total = fo[c, z, sub, :] + vis[c] * beside
                total = total + jnp.where(disk[h], sunk[c], plain[c]) * v
                for d in range(F):
                    if d != c:
                        total = total + mat[c][d] * cen[d][h]
                fo[c, z, sub, :] = total
        return carry

    planes(0, depth, UR, residual_plane, 0)

    ld_lower.wait()
    ld_upper.wait()
    for c in range(F):
        for h, sub in enumerate(HALF):
            low[c, h] = lo[c, 0, sub, :]
            lo[c, 0, sub, :] = one_tile


    def decay_plane(z, carry):
        new = []
        for i, (p, q, r) in enumerate(carry):
            c, sub = i // 2, HALF[i % 2]
            l, u = lo[c, z, sub, :], up[c, z, sub, :]
            l2 = 1.0 - l * l
            u2 = 1.0 - u * u
            g = u2 * lax.rsqrt(u2)
            gl[c, z, sub, :] = l2 * lax.rsqrt(l2)
            gu[c, z, sub, :] = g
            p = p * l
            w = q * g
            pp[c, z, sub, :] = p
            qg[c, z, sub, :] = w
            new.append((p, q * u, r + w * p))
        return tuple(new)

    acd = planes(0, depth, UE, decay_plane, ((one_tile, one_tile, zero_tile),) * NV)
    for c in range(F):
        for h, sub in enumerate(HALF):
            l2 = 1.0 - low[c, h] * low[c, h]
            gl[c, 0, sub, :] = l2 * lax.rsqrt(l2)
            p, q, r = acd[2 * c + h]
            acd_s[2 * c + h, 0] = p * low[c, h]
            acd_s[2 * c + h, 1] = q
            acd_s[2 * c + h, 2] = r * low[c, h]

    pl.semaphore_wait(row_sem, NXC - 1)

    other = mb + 1 - 2 * core
    pl.semaphore_signal(pair_sem, inc=1, device_id={"blk": other})
    pl.semaphore_wait(pair_sem, 1)

    def drain(ref, sem):
        copy(ref, ref, sem).wait()

    def to_solvers(src, dst, ssem, rsem):
        for mine in range(2):

            @pl.when(core == mine)
            def _():
                for v, (line, at) in enumerate(SOLVERS[mine]):
                    out = pltpu.make_async_remote_copy(
                        src_ref=src.at[v], dst_ref=dst.at[me], send_sem=ssem, recv_sem=rsem,
                        device_id={"line": line, "blk": mb if at == mine else other},
                    )
                    if at == mine:
                        pl.when(me != line)(out.start)
                    else:
                        out.start()

    to_solvers(acd_s, acd_r, acd_ssem, acd_rsem)

    def source(z, i):
        c, sub = i // 2, HALF[i % 2]
        src = bi[c, 0, z, sub, :] * fo[0, z, sub, :]
        for d in range(1, F):
            src = src + bi[c, d, z, sub, :] * fo[d, z, sub, :]
        return gl[c, z, sub, :] * src

    def sweep_plane(z, carry):
        s, e = carry
        new_s, new_e = [], []
        for i in range(NV):
            c, sub = i // 2, HALF[i % 2]
            v = lo[c, z, sub, :] * s[i] + source(z, i)
            sw[c, z, sub, :] = v
            new_s.append(v)
            new_e.append(e[i] + qg[c, z, sub, :] * v)
        return tuple(new_s), tuple(new_e)

    def add_x(side, part, row):
        zs = slice(part * piece, part * piece + piece)
        for c in range(F):
            fo[c, zs, row, :] = fo[c, zs, row, :] + vis[c] * xh[side, c, zs]

    def add_z(side, z):
        for c in range(F):
            fo[c, z] = fo[c, z] + vis[c] * zh[side, c]

    def x_halo(part):
        @pl.when(has_left)
        def _():
            x_send(1, part).wait_recv()
            add_x(0, part, 0)

        @pl.when(has_right)
        def _():
            x_send(0, part).wait_recv()
            add_x(1, part, 15)

    carry = ((zero_tile,) * NV, (zero_tile,) * NV)
    for k in range(CH):
        if k * step % piece == 0:
            x_halo(k * step // piece)
        ld_binv(k).wait()
        begin = max(k * step, 1)
        end = min((k + 1) * step, depth - 1)
        carry = planes(begin, end - begin, US, sweep_plane, carry)

    @pl.when(has_high)
    def _():
        z_send(0).wait_recv()
        add_z(1, depth - 1)

    s_all, e_all = sweep_plane(depth - 1, carry)

    @pl.when(has_low)
    def _():
        z_send(1).wait_recv()
        add_z(0, 0)

    for i in range(NV):
        c, h = i // 2, i % 2
        p, q, r = acd[i]
        s0 = source(0, i)
        be_s[i, 0] = s_all[i] + p * s0
        be_s[i, 1] = e_all[i] + r * s0
        ret[c, h, 0] = s0
    to_solvers(be_s, be_r, be_ssem, be_rsem)

    def down_plane(z, carry):
        new = []
        for i, (u, r, v) in enumerate(carry):
            c, sub = i // 2, HALF[i % 2]
            a, g = up[c, z, sub, :], gu[c, z, sub, :]
            u = a * u + g * sw[c, z, sub, :]
            r = a * r + g * pp[c, z, sub, :]
            v = a * v
            u0[c, z, sub, :] = u
            rr[c, z, sub, :] = r
            vv[c, z, sub, :] = v
            new.append((u, r, v))
        return tuple(new)

    planes(depth - 1, depth, UB, down_plane, ((zero_tile, zero_tile, one_tile),) * NV, down=True)

    def role(cross):
        found, tile = False, 0
        for mine in range(2):
            for v, (line, at) in enumerate(SOLVERS[mine]):
                if (at != mine) == cross:
                    here = jnp.logical_and(core == at, me == line)
                    found = jnp.logical_or(found, here)
                    tile = jnp.where(here, v, tile)
        return found, tile

    def solve(tile, cross):
        count = n_line if cross else n_line - 1
        if not cross:
            acd_r[me] = acd_s[tile]
            be_r[me] = be_s[tile]
        drain(acd_r.at[pl.ds(0, count)], acd_rsem)
        drain(be_r.at[pl.ds(0, count)], be_rsem)
        s = zero_tile
        t = []
        for k in range(n_line):
            ret_s[k, 0] = s
            t.append(acd_r[k, 2] * s + be_r[k, 1])
            s = acd_r[k, 0] * s + be_r[k, 0]
        u = zero_tile
        for k in range(n_line - 1, -1, -1):
            ret_s[k, 1] = u
            u = acd_r[k, 1] * u + t[k]
        for k in ORDER:
            out = pltpu.make_async_remote_copy(
                src_ref=ret_s.at[k], dst_ref=ret_r.at[tile], send_sem=ret_ssem, recv_sem=ret_rsem,
                device_id={"line": k, "blk": other if cross else mb},
            )
            if cross:
                out.start()
            else:
                pl.when(me != k)(out.start)
        if not cross:
            ret_r[tile] = ret_s[me]

    solves_other, other_tile = role(True)
    solves_own, own_tile = role(False)

    @pl.when(solves_other)
    def _():
        solve(other_tile, True)
        drain(ret_s, ret_ssem)

    @pl.when(solves_own)
    def _():
        solve(own_tile, False)
        drain(ret_r.at[pl.ds(0, NV - 1)], ret_rsem)
        drain(ret_s.at[pl.ds(0, n_line - 1)], ret_ssem)
        drain(acd_s.at[pl.ds(0, NV - 1)], acd_ssem)
        drain(be_s.at[pl.ds(0, NV - 1)], be_ssem)

    @pl.when(jnp.logical_not(solves_own))
    def _():
        drain(ret_r, ret_rsem)
        drain(acd_s, acd_ssem)
        drain(be_s, be_ssem)

    for c in range(F):
        for h in range(2):
            ret[c, h, 0] = ret[c, h, 0] + low[c, h] * ret_r[2 * c + h, 0]
            ret[c, h, 1] = ret_r[2 * c + h, 1]

    for cond, out in outgoing:
        pl.when(cond)(out.wait_send)


def finish_kernel(u0, rr, vv, fo, ret, update_h, resid_h, out, res_sem, out_sem):
    depth = u0.shape[1]
    step = depth // CF
    write_res = pltpu.make_async_copy(fo, resid_h, res_sem)
    write_res.start()

    def update_copy(k):
        part = pl.ds(k * step, step)
        return pltpu.make_async_copy(out.at[:, part], update_h.at[:, part], out_sem.at[k])

    s_in = tiles(lambda c, h: ret[c, h, 0])
    u_in = tiles(lambda c, h: ret[c, h, 1])

    def plane(z, carry):
        for i in range(NV):
            c, sub = i // 2, HALF[i % 2]
            out[c, z, sub, :] = u0[c, z, sub, :] + rr[c, z, sub, :] * s_in[i] + vv[c, z, sub, :] * u_in[i]
        return carry

    for k in range(CF):
        planes(k * step, step, UF, plane, 0)
        update_copy(k).start()
    write_res.wait()
    for k in range(CF):
        update_copy(k).wait()


def local(
    state, forcing, viscosity, coupling, thrust, disk_mask, block_inverse, lower_decay, upper_decay
):
    fields, depth, width, lanes = state.shape
    n_line = lax.axis_size("line")
    full = (fields, depth, width, lanes)
    f32 = jnp.float32
    V = pltpu.VMEM
    dma = pltpu.SemaphoreType.DMA
    hbm = pl.BlockSpec(memory_space=pltpu.HBM)
    vmem = pl.BlockSpec(memory_space=pltpu.VMEM)
    args = (viscosity, coupling, thrust, state, forcing, disk_mask, block_inverse, lower_decay, upper_decay)
    parts = pl.pallas_call(
        segment_kernel,
        out_shape=(V(full, f32),) * 4 + (V((fields, 2, 2, 8, lanes), f32),),
        in_specs=[hbm] * len(args),
        out_specs=(vmem,) * 5,
        scratch_shapes=[
            V((fields, depth + 2, width, lanes), f32),
            V((depth, width, lanes), jnp.int32),
            V((fields,) + full, f32),
            V(full, f32),
            V(full, f32),
            V(full, f32),
            V(full, f32),
            V(full, f32),
            V(full, f32),
            V(full, f32),
            pltpu.SMEM((fields,), f32),
            pltpu.SMEM((fields, fields), f32),
            pltpu.SMEM((fields,), f32),
            V((2, fields, depth, lanes), f32),
            V((2, fields, depth, lanes), f32),
            V((2, fields, width, lanes), f32),
            V((fields, 2, 8, lanes), f32),
            V((NV, 3, 8, lanes), f32),
            V((n_line, 3, 8, lanes), f32),
            V((NV, 2, 8, lanes), f32),
            V((n_line, 2, 8, lanes), f32),
            V((n_line, 2, 8, lanes), f32),
            V((NV, 2, 8, lanes), f32),
            dma((3,)),
            dma((5,)),
            dma((CF,)),
            dma((2 + 2 * XP,)),
            dma((2 + 2 * XP,)),
            dma, dma, dma, dma, dma, dma,
            pltpu.SemaphoreType.REGULAR,
            pltpu.SemaphoreType.REGULAR,
        ],
        compiler_params=pltpu.CompilerParams(
            collective_id=0, has_side_effects=True, vmem_limit_bytes=40 * 1024 * 1024
        ),
    )(*(pltpu.with_memory_space_constraint(x, pltpu.HBM) for x in args))
    return pl.pallas_call(
        finish_kernel,
        out_shape=(pltpu.HBM(full, f32), pltpu.HBM(full, f32)),
        in_specs=[vmem] * 5,
        out_specs=(hbm, hbm),
        scratch_shapes=[V(full, f32), dma, dma((CF,))],
        compiler_params=pltpu.CompilerParams(vmem_limit_bytes=16 * 1024 * 1024),
    )(*(pltpu.with_memory_space_constraint(x, pltpu.VMEM) for x in parts))


def solution(mesh):
    in_specs = (
        P(None, "line", "blk", None),
        P(None, "line", "blk", None),
        P(),
        P(),
        P(),
        P("line", "blk", None),
        P(None, None, "line", "blk", None),
        P(None, "line", "blk", None),
        P(None, "line", "blk", None),
    )
    out_specs = (P(None, "line", "blk", None), P(None, "line", "blk", None))
    return jax.shard_map(local, mesh=mesh, in_specs=in_specs, out_specs=out_specs, check_vma=False)
```

```python
import jax
import jax.numpy as jnp
from jax import lax
from jax.experimental import pallas as pl
from jax.experimental.pallas import tpu as pltpu
from jax.sharding import PartitionSpec as P

F = 5
NV = 2 * F
CH = 4
UE = 4
UR = 8
US = 4
UB = 4
UF = 2
CF = 4
HALF = (slice(0, 8), slice(8, 16))
NXC = NYC = 4
SOLVERS = (
    ((3, 1), (12, 1), (9, 1), (5, 1), (13, 1), (6, 1), (8, 0), (7, 0), (0, 0), (4, 0)),
    ((0, 1), (4, 1), (12, 1), (15, 1), (3, 1), (8, 1), (1, 1), (2, 1), (11, 1), (7, 1)),
)
ORDER = (0, 1, 4, 3, 12, 2, 8, 5, 13, 7, 6, 9, 15, 14, 11, 10)


def planes(begin, count, unroll, body, carry, down=False):
    def one(z, carry):
        return body(begin - z if down else begin + z, carry)

    def some(i, carry):
        for j in range(unroll):
            carry = one(i * unroll + j, carry)
        return carry

    carry = lax.fori_loop(0, count // unroll, some, carry)
    for z in range(count - count % unroll, count):
        carry = one(z, carry)
    return carry


def tiles(fn):
    return tuple(fn(c, h) for c in range(F) for h in range(2))


def segment_kernel(
    visc_h, coup_h, thr_h, state_h, forcing_h, mask_h, binv_h, lower_h, upper_h,
    u0, rr, vv, fo, ret,
    st, mk, bi, lo, up, gl, gu, qg, pp, sw,
    visc, coup, thr, xs, xh, zh, low, acd_s, acd_r, be_s, be_r, ret_s, ret_r,
    small_sem, load_sem, binv_sem, halo_ssem, halo_rsem,
    acd_ssem, acd_rsem, be_ssem, be_rsem, ret_ssem, ret_rsem, row_sem, pair_sem,
):
    n_line = lax.axis_size("line")
    n_blk = lax.axis_size("blk")
    me = lax.axis_index("line")
    mb = lax.axis_index("blk")
    x, y, core = me // NYC, me % NYC, mb % 2
    depth = lo.shape[1]
    step = depth // CH

    copy = pltpu.make_async_copy
    ld_state = copy(state_h, st.at[:, pl.ds(1, depth)], load_sem.at[0])
    ld_forcing = copy(forcing_h, fo, load_sem.at[1])
    ld_mask = copy(mask_h, mk, load_sem.at[2])
    ld_lower = copy(lower_h, lo, load_sem.at[3])
    ld_upper = copy(upper_h, up, load_sem.at[4])
    ld_small = [
        copy(src, dst, small_sem.at[i])
        for i, (src, dst) in enumerate(((visc_h, visc), (coup_h, coup), (thr_h, thr)))
    ]

    def ld_binv(k):
        part = pl.ds(k * step, step)
        return copy(binv_h.at[:, :, part], bi.at[:, :, part], binv_sem.at[k])

    ld_state.start()
    for cp in ld_small:
        cp.start()
    ld_lower.start()
    ld_upper.start()
    ld_forcing.start()
    ld_mask.start()

    has_low, has_high = me > 0, me < n_line - 1
    has_left, has_right = mb > 0, mb < n_blk - 1
    turn_low = jnp.logical_and(has_low, y == 0)
    turn_high = jnp.logical_and(has_high, y == NYC - 1)
    barrier = pltpu.get_barrier_semaphore()

    def greet(**device):
        pl.semaphore_signal(barrier, inc=1, device_id=device)

    def wrap(v, n):
        return jnp.where(v >= n, v - n, v)

    def in_column(d):
        return wrap(x + d, NXC) * NYC + y

    pl.when(has_left)(lambda: greet(blk=mb - 1))
    pl.when(has_right)(lambda: greet(blk=mb + 1))
    pl.when(turn_low)(lambda: greet(line=me - 1))
    pl.when(turn_high)(lambda: greet(line=me + 1))
    for d in range(1, NYC):
        greet(line=x * NYC + wrap(y + d, NYC))
    for d in range(1, NXC):
        greet(line=in_column(d))

    for k in range(CH):
        ld_binv(k).start()

    zero_tile = jnp.zeros((8, 128), jnp.float32)
    one_tile = jnp.ones((8, 128), jnp.float32)
    for c in range(F):
        for sub in HALF:
            st[c, 0, sub, :] = zero_tile
            st[c, depth + 1, sub, :] = zero_tile
            sw[c, 0, sub, :] = zero_tile

    ld_state.wait()
    for c in range(F):
        for side, row in ((0, 0), (1, 15)):
            xs[side, c] = st[c, 1 : depth + 1, row, :]

    greeted = NYC - 1 + NXC - 1
    for cond in (has_left, has_right, turn_low, turn_high):
        greeted = greeted + jnp.where(cond, 1, 0)
    pl.semaphore_wait(barrier, greeted)

    def z_send(side):
        return pltpu.make_async_remote_copy(
            src_ref=st.at[:, depth if side else 1], dst_ref=zh.at[1 - side],
            send_sem=halo_ssem.at[side], recv_sem=halo_rsem.at[side],
            device_id={"line": me + 1 if side else me - 1},
        )

    def x_send(side):
        return pltpu.make_async_remote_copy(
            src_ref=xs.at[side], dst_ref=xh.at[1 - side],
            send_sem=halo_ssem.at[2 + side], recv_sem=halo_rsem.at[2 + side],
            device_id={"blk": mb + 1 if side else mb - 1},
        )

    outgoing = (
        (has_low, z_send(0)),
        (has_high, z_send(1)),
        (has_left, x_send(0)),
        (has_right, x_send(1)),
    )
    for cond, out in outgoing:
        pl.when(cond)(out.start)

    for d in range(1, NXC):
        pl.semaphore_signal(row_sem, inc=1, device_id={"line": in_column(d)})

    ld_lower.wait()
    ld_upper.wait()
    for c in range(F):
        for h, sub in enumerate(HALF):
            low[c, h] = lo[c, 0, sub, :]
            lo[c, 0, sub, :] = one_tile


    def decay_plane(z, carry):
        new = []
        for i, (p, q, r) in enumerate(carry):
            c, sub = i // 2, HALF[i % 2]
            l, u = lo[c, z, sub, :], up[c, z, sub, :]
            l2 = 1.0 - l * l
            u2 = 1.0 - u * u
            g = u2 * lax.rsqrt(u2)
            gl[c, z, sub, :] = l2 * lax.rsqrt(l2)
            gu[c, z, sub, :] = g
            p = p * l
            w = q * g
            pp[c, z, sub, :] = p
            qg[c, z, sub, :] = w
            new.append((p, q * u, r + w * p))
        return tuple(new)

    acd = planes(0, depth, UE, decay_plane, ((one_tile, one_tile, zero_tile),) * NV)
    for c in range(F):
        for h, sub in enumerate(HALF):
            l2 = 1.0 - low[c, h] * low[c, h]
            gl[c, 0, sub, :] = l2 * lax.rsqrt(l2)
            p, q, r = acd[2 * c + h]
            acd_s[2 * c + h, 0] = p * low[c, h]
            acd_s[2 * c + h, 1] = q
            acd_s[2 * c + h, 2] = r * low[c, h]

    ld_forcing.wait()
    ld_mask.wait()
    for cp in ld_small:
        cp.wait()
    rows = lax.broadcasted_iota(jnp.int32, (8, 128), 0)
    first = rows == 0
    last = rows == 7
    vis = [visc[c] for c in range(F)]
    mat = [[-coup[c, d] for d in range(F)] for c in range(F)]
    plain = [mat[c][c] - 6.0 * vis[c] for c in range(F)]
    sunk = [plain[c] - thr[c] for c in range(F)]

    def residual_plane(z, carry):
        cen = [[st[c, z + 1, sub, :] for sub in HALF] for c in range(F)]
        disk = [mk[z, sub, :] != 0 for sub in HALF]
        for c in range(F):
            v0, v1 = cen[c]
            r0, r1 = pltpu.roll(v0, 1, 0), pltpu.roll(v1, 1, 0)
            q0, q1 = pltpu.roll(v0, 7, 0), pltpu.roll(v1, 7, 0)
            xsum = (
                jnp.where(first, 0.0, r0) + jnp.where(last, q1, q0),
                jnp.where(first, r0, r1) + jnp.where(last, 0.0, q1),
            )
            for h, sub in enumerate(HALF):
                v = cen[c][h]
                beside = (st[c, z, sub, :] + st[c, z + 2, sub, :]) + xsum[h]
                beside = beside + (pltpu.roll(v, 1, 1) + pltpu.roll(v, 127, 1))
                total = fo[c, z, sub, :] + vis[c] * beside
                total = total + jnp.where(disk[h], sunk[c], plain[c]) * v
                for d in range(F):
                    if d != c:
                        total = total + mat[c][d] * cen[d][h]
                fo[c, z, sub, :] = total
        return carry

    planes(0, depth // 2, UR, residual_plane, 0)

    pl.semaphore_wait(row_sem, NXC - 1)

    other = mb + 1 - 2 * core
    pl.semaphore_signal(pair_sem, inc=1, device_id={"blk": other})
    pl.semaphore_wait(pair_sem, 1)

    def drain(ref, sem):
        copy(ref, ref, sem).wait()

    def to_solvers(src, dst, ssem, rsem):
        for mine in range(2):

            @pl.when(core == mine)
            def _():
                for v, (line, at) in enumerate(SOLVERS[mine]):
                    out = pltpu.make_async_remote_copy(
                        src_ref=src.at[v], dst_ref=dst.at[int(at == mine), me], send_sem=ssem,
                        recv_sem=rsem.at[int(at == mine)],
                        device_id={"line": line, "blk": mb if at == mine else other},
                    )
                    if at == mine:
                        pl.when(me != line)(out.start)
                    else:
                        out.start()

    to_solvers(acd_s, acd_r, acd_ssem, acd_rsem)

    planes(depth // 2, depth // 2, UR, residual_plane, 0)

    def source(z, c, sub):
        src = bi[c, 0, z, sub, :] * fo[0, z, sub, :]
        for d in range(1, F):
            src = src + bi[c, d, z, sub, :] * fo[d, z, sub, :]
        return gl[c, z, sub, :] * src

    def sweep_plane(z, carry, sub):
        new = []
        for c, (s, e) in enumerate(carry):
            v = lo[c, z, sub, :] * s + source(z, c, sub)
            sw[c, z, sub, :] = v
            new.append((v, e + qg[c, z, sub, :] * v))
        return tuple(new)

    def add_x(side, row):
        for c in range(F):
            fo[c, :, row, :] = fo[c, :, row, :] + vis[c] * xh[side, c]

    def add_z(side, z):
        for c in range(F):
            fo[c, z] = fo[c, z] + vis[c] * zh[side, c]

    def sweep_half(turn, unused):
        h = jnp.where(core == 1, turn, 1 - turn)
        sub = pl.ds(pl.multiple_of(8 * h, 8), 8)

        @pl.when(jnp.logical_and(h == 0, has_left))
        def _():
            x_send(1).wait_recv()
            add_x(0, 0)

        @pl.when(jnp.logical_and(h == 1, has_right))
        def _():
            x_send(0).wait_recv()
            add_x(1, 15)

        carry = ((zero_tile, zero_tile),) * F
        for k in range(CH):
            pl.when(turn == 0)(ld_binv(k).wait)
            begin = max(k * step, 1)
            end = min((k + 1) * step, depth - 1)
            carry = planes(begin, end - begin, US, lambda z, c: sweep_plane(z, c, sub), carry)
        for c in range(F):
            be_s[2 * c + h, 0] = carry[c][0]
            be_s[2 * c + h, 1] = carry[c][1]
        return unused

    lax.fori_loop(0, 2, sweep_half, 0)

    @pl.when(has_high)
    def _():
        z_send(0).wait_recv()
        add_z(1, depth - 1)

    @pl.when(has_low)
    def _():
        z_send(1).wait_recv()
        add_z(0, 0)

    for h, sub in enumerate(HALF):
        carry = tuple((be_s[2 * c + h, 0], be_s[2 * c + h, 1]) for c in range(F))
        carry = sweep_plane(depth - 1, carry, sub)
        for c in range(F):
            p, q, r = acd[2 * c + h]
            s0 = source(0, c, sub)
            be_s[2 * c + h, 0] = carry[c][0] + p * s0
            be_s[2 * c + h, 1] = carry[c][1] + r * s0
            ret[c, h, 0] = s0
    to_solvers(be_s, be_r, be_ssem, be_rsem)

    def down_plane(z, carry):
        new = []
        for i, (u, r, v) in enumerate(carry):
            c, sub = i // 2, HALF[i % 2]
            a, g = up[c, z, sub, :], gu[c, z, sub, :]
            u = a * u + g * sw[c, z, sub, :]
            r = a * r + g * pp[c, z, sub, :]
            v = a * v
            u0[c, z, sub, :] = u
            rr[c, z, sub, :] = r
            vv[c, z, sub, :] = v
            new.append((u, r, v))
        return tuple(new)

    planes(depth - 1, depth, UB, down_plane, ((zero_tile, zero_tile, one_tile),) * NV, down=True)

    def role(cross):
        found, tile = False, 0
        for mine in range(2):
            for v, (line, at) in enumerate(SOLVERS[mine]):
                if (at != mine) == cross:
                    here = jnp.logical_and(core == at, me == line)
                    found = jnp.logical_or(found, here)
                    tile = jnp.where(here, v, tile)
        return found, tile

    def solve(tile, cross):
        i = 0 if cross else 1
        count = n_line if cross else n_line - 1
        if not cross:
            acd_r[i, me] = acd_s[tile]
            be_r[i, me] = be_s[tile]
        drain(acd_r.at[i, pl.ds(0, count)], acd_rsem.at[i])
        drain(be_r.at[i, pl.ds(0, count)], be_rsem.at[i])
        s = zero_tile
        t = []
        for k in range(n_line):
            ret_s[i, k, 0] = s
            t.append(acd_r[i, k, 2] * s + be_r[i, k, 1])
            s = acd_r[i, k, 0] * s + be_r[i, k, 0]
        u = zero_tile
        for k in range(n_line - 1, -1, -1):
            ret_s[i, k, 1] = u
            u = acd_r[i, k, 1] * u + t[k]
        for k in ORDER:
            out = pltpu.make_async_remote_copy(
                src_ref=ret_s.at[i, k], dst_ref=ret_r.at[tile], send_sem=ret_ssem.at[i], recv_sem=ret_rsem,
                device_id={"line": k, "blk": other if cross else mb},
            )
            if cross:
                out.start()
            else:
                pl.when(me != k)(out.start)
        if not cross:
            ret_r[tile] = ret_s[i, me]

    solves_other, other_tile = role(True)
    solves_own, own_tile = role(False)

    @pl.when(solves_own)
    def _():
        solve(own_tile, False)

    @pl.when(solves_other)
    def _():
        solve(other_tile, True)

    @pl.when(solves_own)
    def _():
        drain(ret_r.at[pl.ds(0, NV - 1)], ret_rsem)
        drain(acd_s.at[pl.ds(0, NV - 1)], acd_ssem)
        drain(be_s.at[pl.ds(0, NV - 1)], be_ssem)

    @pl.when(jnp.logical_not(solves_own))
    def _():
        drain(ret_r, ret_rsem)
        drain(acd_s, acd_ssem)
        drain(be_s, be_ssem)

    for c in range(F):
        for h in range(2):
            ret[c, h, 0] = ret[c, h, 0] + low[c, h] * ret_r[2 * c + h, 0]
            ret[c, h, 1] = ret_r[2 * c + h, 1]

    for cond, out in outgoing:
        pl.when(cond)(out.wait_send)
    pl.when(solves_other)(lambda: drain(ret_s.at[0], ret_ssem.at[0]))
    pl.when(solves_own)(lambda: drain(ret_s.at[1, pl.ds(0, n_line - 1)], ret_ssem.at[1]))


def finish_kernel(u0, rr, vv, fo, ret, update_h, resid_h, out, res_sem, out_sem):
    depth = u0.shape[1]
    step = depth // CF
    write_res = pltpu.make_async_copy(fo, resid_h, res_sem)
    write_res.start()

    def update_copy(k):
        part = pl.ds(k * step, step)
        return pltpu.make_async_copy(out.at[:, part], update_h.at[:, part], out_sem.at[k])

    s_in = tiles(lambda c, h: ret[c, h, 0])
    u_in = tiles(lambda c, h: ret[c, h, 1])

    def plane(z, carry):
        for i in range(NV):
            c, sub = i // 2, HALF[i % 2]
            out[c, z, sub, :] = u0[c, z, sub, :] + rr[c, z, sub, :] * s_in[i] + vv[c, z, sub, :] * u_in[i]
        return carry

    for k in range(CF):
        planes(k * step, step, UF, plane, 0)
        update_copy(k).start()
    write_res.wait()
    for k in range(CF):
        update_copy(k).wait()


def local(
    state, forcing, viscosity, coupling, thrust, disk_mask, block_inverse, lower_decay, upper_decay
):
    fields, depth, width, lanes = state.shape
    n_line = lax.axis_size("line")
    full = (fields, depth, width, lanes)
    f32 = jnp.float32
    V = pltpu.VMEM
    dma = pltpu.SemaphoreType.DMA
    hbm = pl.BlockSpec(memory_space=pltpu.HBM)
    vmem = pl.BlockSpec(memory_space=pltpu.VMEM)
    args = (viscosity, coupling, thrust, state, forcing, disk_mask, block_inverse, lower_decay, upper_decay)
    parts = pl.pallas_call(
        segment_kernel,
        out_shape=(V(full, f32),) * 4 + (V((fields, 2, 2, 8, lanes), f32),),
        in_specs=[hbm] * len(args),
        out_specs=(vmem,) * 5,
        scratch_shapes=[
            V((fields, depth + 2, width, lanes), f32),
            V((depth, width, lanes), jnp.int32),
            V((fields,) + full, f32),
            V(full, f32),
            V(full, f32),
            V(full, f32),
            V(full, f32),
            V(full, f32),
            V(full, f32),
            V(full, f32),
            pltpu.SMEM((fields,), f32),
            pltpu.SMEM((fields, fields), f32),
            pltpu.SMEM((fields,), f32),
            V((2, fields, depth, lanes), f32),
            V((2, fields, depth, lanes), f32),
            V((2, fields, width, lanes), f32),
            V((fields, 2, 8, lanes), f32),
            V((NV, 3, 8, lanes), f32),
            V((2, n_line, 3, 8, lanes), f32),
            V((NV, 2, 8, lanes), f32),
            V((2, n_line, 2, 8, lanes), f32),
            V((2, n_line, 2, 8, lanes), f32),
            V((NV, 2, 8, lanes), f32),
            dma((3,)),
            dma((5,)),
            dma((CF,)),
            dma((4,)),
            dma((4,)),
            dma, dma((2,)), dma, dma((2,)), dma((2,)), dma,
            pltpu.SemaphoreType.REGULAR,
            pltpu.SemaphoreType.REGULAR,
        ],
        compiler_params=pltpu.CompilerParams(
            collective_id=0, has_side_effects=True, vmem_limit_bytes=40 * 1024 * 1024
        ),
    )(*(pltpu.with_memory_space_constraint(x, pltpu.HBM) for x in args))
    return pl.pallas_call(
        finish_kernel,
        out_shape=(pltpu.HBM(full, f32), pltpu.HBM(full, f32)),
        in_specs=[vmem] * 5,
        out_specs=(hbm, hbm),
        scratch_shapes=[V(full, f32), dma, dma((CF,))],
        compiler_params=pltpu.CompilerParams(vmem_limit_bytes=16 * 1024 * 1024),
    )(*(pltpu.with_memory_space_constraint(x, pltpu.VMEM) for x in parts))


def solution(mesh):
    in_specs = (
        P(None, "line", "blk", None),
        P(None, "line", "blk", None),
        P(),
        P(),
        P(),
        P("line", "blk", None),
        P(None, None, "line", "blk", None),
        P(None, "line", "blk", None),
        P(None, "line", "blk", None),
    )
    out_specs = (P(None, "line", "blk", None), P(None, "line", "blk", None))
    return jax.shard_map(local, mesh=mesh, in_specs=in_specs, out_specs=out_specs, check_vma=False)
```

```python
import jax
import jax.numpy as jnp
from jax import lax
from jax.experimental import pallas as pl
from jax.experimental.pallas import tpu as pltpu
from jax.sharding import PartitionSpec as P

F = 5
NV = 2 * F
CH = 4
UE = 4
UR = 8
US = 4
UB = 4
UF = 2
CF = 4
HALF = (slice(0, 8), slice(8, 16))
NXC = NYC = 4
SOLVERS = (
    ((3, 1), (12, 1), (9, 1), (5, 1), (13, 1), (6, 1), (8, 0), (7, 0), (0, 0), (4, 0)),
    ((0, 1), (4, 1), (12, 1), (15, 1), (3, 1), (8, 1), (1, 1), (2, 1), (11, 1), (7, 1)),
)
ORDER = (0, 1, 4, 3, 12, 2, 8, 5, 13, 7, 6, 9, 15, 14, 11, 10)


def planes(begin, count, unroll, body, carry, down=False):
    def one(z, carry):
        return body(begin - z if down else begin + z, carry)

    def some(i, carry):
        for j in range(unroll):
            carry = one(i * unroll + j, carry)
        return carry

    carry = lax.fori_loop(0, count // unroll, some, carry)
    for z in range(count - count % unroll, count):
        carry = one(z, carry)
    return carry


def tiles(fn):
    return tuple(fn(c, h) for c in range(F) for h in range(2))


def segment_kernel(
    visc_h, coup_h, thr_h, state_h, forcing_h, mask_h, binv_h, lower_h, upper_h,
    u0, rr, vv, fo, ret,
    st, mk, bi, lo, up, gl, gu, qg, pp, sw,
    visc, coup, thr, xs, xh, zh, low, acd_s, acd_r, be_s, be_r, ret_s, ret_r,
    small_sem, load_sem, binv_sem, halo_ssem, halo_rsem,
    acd_ssem, acd_rsem, be_ssem, be_rsem, ret_ssem, ret_rsem, row_sem, pair_sem,
):
    n_line = lax.axis_size("line")
    n_blk = lax.axis_size("blk")
    me = lax.axis_index("line")
    mb = lax.axis_index("blk")
    x, y, core = me // NYC, me % NYC, mb % 2
    depth = lo.shape[1]
    step = depth // CH

    copy = pltpu.make_async_copy
    ld_state = copy(state_h, st.at[:, pl.ds(1, depth)], load_sem.at[0])
    ld_forcing = copy(forcing_h, fo, load_sem.at[1])
    ld_mask = copy(mask_h, mk, load_sem.at[2])
    ld_lower = copy(lower_h, lo, load_sem.at[3])
    ld_upper = copy(upper_h, up, load_sem.at[4])
    ld_small = [
        copy(src, dst, small_sem.at[i])
        for i, (src, dst) in enumerate(((visc_h, visc), (coup_h, coup), (thr_h, thr)))
    ]

    def ld_binv(k):
        part = pl.ds(k * step, step)
        return copy(binv_h.at[:, :, part], bi.at[:, :, part], binv_sem.at[k])

    ld_state.start()
    for cp in ld_small:
        cp.start()
    ld_lower.start()
    ld_upper.start()
    ld_forcing.start()
    ld_mask.start()

    has_low, has_high = me > 0, me < n_line - 1
    has_left, has_right = mb > 0, mb < n_blk - 1
    barrier = pltpu.get_barrier_semaphore()

    def greet(**device):
        pl.semaphore_signal(barrier, inc=1, device_id=device)

    def wrap(v, n):
        return jnp.where(v >= n, v - n, v)

    def in_column(d):
        return wrap(x + d, NXC) * NYC + y

    pl.when(has_left)(lambda: greet(blk=mb - 1))
    pl.when(has_right)(lambda: greet(blk=mb + 1))
    pl.when(has_low)(lambda: greet(line=me - 1))
    pl.when(has_high)(lambda: greet(line=me + 1))
    second = mb + 1 - core
    for d in range(1, NYC):
        greet(line=x * NYC + wrap(y + d, NYC), blk=second)

    @pl.when(core == 1)
    def _():
        for d in range(1, NXC):
            greet(line=in_column(d))

    for k in range(CH):
        ld_binv(k).start()

    zero_tile = jnp.zeros((8, 128), jnp.float32)
    one_tile = jnp.ones((8, 128), jnp.float32)
    for c in range(F):
        for sub in HALF:
            st[c, 0, sub, :] = zero_tile
            st[c, depth + 1, sub, :] = zero_tile
            sw[c, 0, sub, :] = zero_tile

    ld_state.wait()
    for c in range(F):
        for side, row in ((0, 0), (1, 15)):
            xs[side, c] = st[c, 1 : depth + 1, row, :]

    greeted = core * (2 * (NYC - 1) + NXC - 1)
    for cond in (has_left, has_right, has_low, has_high):
        greeted = greeted + jnp.where(cond, 1, 0)
    pl.semaphore_wait(barrier, greeted)

    def z_send(side):
        return pltpu.make_async_remote_copy(
            src_ref=st.at[:, depth if side else 1], dst_ref=zh.at[1 - side],
            send_sem=halo_ssem.at[side], recv_sem=halo_rsem.at[side],
            device_id={"line": me + 1 if side else me - 1},
        )

    def x_send(side):
        return pltpu.make_async_remote_copy(
            src_ref=xs.at[side], dst_ref=xh.at[1 - side],
            send_sem=halo_ssem.at[2 + side], recv_sem=halo_rsem.at[2 + side],
            device_id={"blk": mb + 1 if side else mb - 1},
        )

    outgoing = (
        (has_low, z_send(0)),
        (has_high, z_send(1)),
        (has_left, x_send(0)),
        (has_right, x_send(1)),
    )
    for cond, out in outgoing:
        pl.when(cond)(out.start)

    @pl.when(core == 1)
    def _():
        for d in range(1, NXC):
            pl.semaphore_signal(row_sem, inc=1, device_id={"line": in_column(d)})

    ld_lower.wait()
    ld_upper.wait()
    for c in range(F):
        for h, sub in enumerate(HALF):
            low[c, h] = lo[c, 0, sub, :]
            lo[c, 0, sub, :] = one_tile


    def decay_plane(z, carry):
        new = []
        for i, (p, q, r) in enumerate(carry):
            c, sub = i // 2, HALF[i % 2]
            l, u = lo[c, z, sub, :], up[c, z, sub, :]
            l2 = 1.0 - l * l
            u2 = 1.0 - u * u
            g = u2 * lax.rsqrt(u2)
            gl[c, z, sub, :] = l2 * lax.rsqrt(l2)
            gu[c, z, sub, :] = g
            p = p * l
            w = q * g
            pp[c, z, sub, :] = p
            qg[c, z, sub, :] = w
            new.append((p, q * u, r + w * p))
        return tuple(new)

    acd = planes(0, depth, UE, decay_plane, ((one_tile, one_tile, zero_tile),) * NV)
    for c in range(F):
        for h, sub in enumerate(HALF):
            l2 = 1.0 - low[c, h] * low[c, h]
            gl[c, 0, sub, :] = l2 * lax.rsqrt(l2)
            p, q, r = acd[2 * c + h]
            acd_s[2 * c + h, 0] = p * low[c, h]
            acd_s[2 * c + h, 1] = q
            acd_s[2 * c + h, 2] = r * low[c, h]

    ld_forcing.wait()
    ld_mask.wait()
    for cp in ld_small:
        cp.wait()
    rows = lax.broadcasted_iota(jnp.int32, (8, 128), 0)
    first = rows == 0
    last = rows == 7
    vis = [visc[c] for c in range(F)]
    mat = [[-coup[c, d] for d in range(F)] for c in range(F)]
    plain = [mat[c][c] - 6.0 * vis[c] for c in range(F)]
    sunk = [plain[c] - thr[c] for c in range(F)]

    def residual_plane(z, carry):
        cen = [[st[c, z + 1, sub, :] for sub in HALF] for c in range(F)]
        disk = [mk[z, sub, :] != 0 for sub in HALF]
        for c in range(F):
            v0, v1 = cen[c]
            r0, r1 = pltpu.roll(v0, 1, 0), pltpu.roll(v1, 1, 0)
            q0, q1 = pltpu.roll(v0, 7, 0), pltpu.roll(v1, 7, 0)
            xsum = (
                jnp.where(first, 0.0, r0) + jnp.where(last, q1, q0),
                jnp.where(first, r0, r1) + jnp.where(last, 0.0, q1),
            )
            for h, sub in enumerate(HALF):
                v = cen[c][h]
                beside = (st[c, z, sub, :] + st[c, z + 2, sub, :]) + xsum[h]
                beside = beside + (pltpu.roll(v, 1, 1) + pltpu.roll(v, 127, 1))
                total = fo[c, z, sub, :] + vis[c] * beside
                total = total + jnp.where(disk[h], sunk[c], plain[c]) * v
                for d in range(F):
                    if d != c:
                        total = total + mat[c][d] * cen[d][h]
                fo[c, z, sub, :] = total
        return carry

    planes(0, depth // 2, UR, residual_plane, 0)

    other = mb + 1 - 2 * core

    @pl.when(core == 1)
    def _():
        pl.semaphore_wait(row_sem, NXC - 1)
        pl.semaphore_signal(pair_sem, inc=1, device_id={"blk": other})

    planes(depth // 2, depth // 2, UR, residual_plane, 0)

    @pl.when(core == 0)
    def _():
        pl.semaphore_wait(pair_sem, 1)


    def drain(ref, sem):
        copy(ref, ref, sem).wait()

    def to_solvers(src, dst, ssem, rsem):
        for mine in range(2):

            @pl.when(core == mine)
            def _():
                for v, (line, at) in enumerate(SOLVERS[mine]):
                    out = pltpu.make_async_remote_copy(
                        src_ref=src.at[v], dst_ref=dst.at[int(at == mine), me], send_sem=ssem,
                        recv_sem=rsem.at[int(at == mine)],
                        device_id={"line": line, "blk": mb if at == mine else other},
                    )
                    if at == mine:
                        pl.when(me != line)(out.start)
                    else:
                        out.start()

    to_solvers(acd_s, acd_r, acd_ssem, acd_rsem)

    def source(z, c, sub):
        src = bi[c, 0, z, sub, :] * fo[0, z, sub, :]
        for d in range(1, F):
            src = src + bi[c, d, z, sub, :] * fo[d, z, sub, :]
        return gl[c, z, sub, :] * src

    def sweep_plane(z, carry, sub):
        new = []
        for c, (s, e) in enumerate(carry):
            v = lo[c, z, sub, :] * s + source(z, c, sub)
            sw[c, z, sub, :] = v
            new.append((v, e + qg[c, z, sub, :] * v))
        return tuple(new)

    def add_x(side, row):
        for c in range(F):
            fo[c, :, row, :] = fo[c, :, row, :] + vis[c] * xh[side, c]

    def add_z(side, z):
        for c in range(F):
            fo[c, z] = fo[c, z] + vis[c] * zh[side, c]

    def sweep_half(turn, unused):
        h = jnp.where(core == 1, turn, 1 - turn)
        sub = pl.ds(pl.multiple_of(8 * h, 8), 8)

        @pl.when(jnp.logical_and(h == 0, has_left))
        def _():
            x_send(1).wait_recv()
            add_x(0, 0)

        @pl.when(jnp.logical_and(h == 1, has_right))
        def _():
            x_send(0).wait_recv()
            add_x(1, 15)

        carry = ((zero_tile, zero_tile),) * F
        for k in range(CH):
            pl.when(turn == 0)(ld_binv(k).wait)
            begin = max(k * step, 1)
            end = min((k + 1) * step, depth - 1)
            carry = planes(begin, end - begin, US, lambda z, c: sweep_plane(z, c, sub), carry)
        for c in range(F):
            be_s[2 * c + h, 0] = carry[c][0]
            be_s[2 * c + h, 1] = carry[c][1]
        return unused

    lax.fori_loop(0, 2, sweep_half, 0)

    @pl.when(has_high)
    def _():
        z_send(0).wait_recv()
        add_z(1, depth - 1)

    @pl.when(has_low)
    def _():
        z_send(1).wait_recv()
        add_z(0, 0)

    for h, sub in enumerate(HALF):
        carry = tuple((be_s[2 * c + h, 0], be_s[2 * c + h, 1]) for c in range(F))
        carry = sweep_plane(depth - 1, carry, sub)
        for c in range(F):
            p, q, r = acd[2 * c + h]
            s0 = source(0, c, sub)
            be_s[2 * c + h, 0] = carry[c][0] + p * s0
            be_s[2 * c + h, 1] = carry[c][1] + r * s0
            ret[c, h, 0] = s0
    to_solvers(be_s, be_r, be_ssem, be_rsem)

    def down_plane(z, carry):
        new = []
        for i, (u, r, v) in enumerate(carry):
            c, sub = i // 2, HALF[i % 2]
            a, g = up[c, z, sub, :], gu[c, z, sub, :]
            u = a * u + g * sw[c, z, sub, :]
            r = a * r + g * pp[c, z, sub, :]
            v = a * v
            u0[c, z, sub, :] = u
            rr[c, z, sub, :] = r
            vv[c, z, sub, :] = v
            new.append((u, r, v))
        return tuple(new)

    planes(depth - 1, depth, UB, down_plane, ((zero_tile, zero_tile, one_tile),) * NV, down=True)

    def role(cross):
        found, tile = False, 0
        for mine in range(2):
            for v, (line, at) in enumerate(SOLVERS[mine]):
                if (at != mine) == cross:
                    here = jnp.logical_and(core == at, me == line)
                    found = jnp.logical_or(found, here)
                    tile = jnp.where(here, v, tile)
        return found, tile

    def solve(tile, cross):
        i = 0 if cross else 1
        count = n_line if cross else n_line - 1
        if not cross:
            acd_r[i, me] = acd_s[tile]
            be_r[i, me] = be_s[tile]
        drain(acd_r.at[i, pl.ds(0, count)], acd_rsem.at[i])
        drain(be_r.at[i, pl.ds(0, count)], be_rsem.at[i])
        s = zero_tile
        t = []
        for k in range(n_line):
            ret_s[i, k, 0] = s
            t.append(acd_r[i, k, 2] * s + be_r[i, k, 1])
            s = acd_r[i, k, 0] * s + be_r[i, k, 0]
        u = zero_tile
        for k in range(n_line - 1, -1, -1):
            ret_s[i, k, 1] = u
            u = acd_r[i, k, 1] * u + t[k]
        for k in ORDER:
            out = pltpu.make_async_remote_copy(
                src_ref=ret_s.at[i, k], dst_ref=ret_r.at[tile], send_sem=ret_ssem.at[i], recv_sem=ret_rsem,
                device_id={"line": k, "blk": other if cross else mb},
            )
            if cross:
                out.start()
            else:
                pl.when(me != k)(out.start)
        if not cross:
            ret_r[tile] = ret_s[i, me]

    solves_other, other_tile = role(True)
    solves_own, own_tile = role(False)

    @pl.when(solves_own)
    def _():
        solve(own_tile, False)

    @pl.when(solves_other)
    def _():
        solve(other_tile, True)

    @pl.when(solves_own)
    def _():
        drain(ret_r.at[pl.ds(0, NV - 1)], ret_rsem)
        drain(acd_s.at[pl.ds(0, NV - 1)], acd_ssem)
        drain(be_s.at[pl.ds(0, NV - 1)], be_ssem)

    @pl.when(jnp.logical_not(solves_own))
    def _():
        drain(ret_r, ret_rsem)
        drain(acd_s, acd_ssem)
        drain(be_s, be_ssem)

    for c in range(F):
        for h in range(2):
            ret[c, h, 0] = ret[c, h, 0] + low[c, h] * ret_r[2 * c + h, 0]
            ret[c, h, 1] = ret_r[2 * c + h, 1]

    for cond, out in outgoing:
        pl.when(cond)(out.wait_send)
    pl.when(solves_other)(lambda: drain(ret_s.at[0], ret_ssem.at[0]))
    pl.when(solves_own)(lambda: drain(ret_s.at[1, pl.ds(0, n_line - 1)], ret_ssem.at[1]))


def finish_kernel(u0, rr, vv, fo, ret, update_h, resid_h, out, res_sem, out_sem):
    depth = u0.shape[1]
    step = depth // CF
    write_res = pltpu.make_async_copy(fo, resid_h, res_sem)
    write_res.start()

    def update_copy(k):
        part = pl.ds(k * step, step)
        return pltpu.make_async_copy(out.at[:, part], update_h.at[:, part], out_sem.at[k])

    s_in = tiles(lambda c, h: ret[c, h, 0])
    u_in = tiles(lambda c, h: ret[c, h, 1])

    def plane(z, carry):
        for i in range(NV):
            c, sub = i // 2, HALF[i % 2]
            out[c, z, sub, :] = u0[c, z, sub, :] + rr[c, z, sub, :] * s_in[i] + vv[c, z, sub, :] * u_in[i]
        return carry

    for k in range(CF):
        planes(k * step, step, UF, plane, 0)
        update_copy(k).start()
    write_res.wait()
    for k in range(CF):
        update_copy(k).wait()


def local(
    state, forcing, viscosity, coupling, thrust, disk_mask, block_inverse, lower_decay, upper_decay
):
    fields, depth, width, lanes = state.shape
    n_line = lax.axis_size("line")
    full = (fields, depth, width, lanes)
    f32 = jnp.float32
    V = pltpu.VMEM
    dma = pltpu.SemaphoreType.DMA
    hbm = pl.BlockSpec(memory_space=pltpu.HBM)
    vmem = pl.BlockSpec(memory_space=pltpu.VMEM)
    args = (viscosity, coupling, thrust, state, forcing, disk_mask, block_inverse, lower_decay, upper_decay)
    parts = pl.pallas_call(
        segment_kernel,
        out_shape=(V(full, f32),) * 4 + (V((fields, 2, 2, 8, lanes), f32),),
        in_specs=[hbm] * len(args),
        out_specs=(vmem,) * 5,
        scratch_shapes=[
            V((fields, depth + 2, width, lanes), f32),
            V((depth, width, lanes), jnp.int32),
            V((fields,) + full, f32),
            V(full, f32),
            V(full, f32),
            V(full, f32),
            V(full, f32),
            V(full, f32),
            V(full, f32),
            V(full, f32),
            pltpu.SMEM((fields,), f32),
            pltpu.SMEM((fields, fields), f32),
            pltpu.SMEM((fields,), f32),
            V((2, fields, depth, lanes), f32),
            V((2, fields, depth, lanes), f32),
            V((2, fields, width, lanes), f32),
            V((fields, 2, 8, lanes), f32),
            V((NV, 3, 8, lanes), f32),
            V((2, n_line, 3, 8, lanes), f32),
            V((NV, 2, 8, lanes), f32),
            V((2, n_line, 2, 8, lanes), f32),
            V((2, n_line, 2, 8, lanes), f32),
            V((NV, 2, 8, lanes), f32),
            dma((3,)),
            dma((5,)),
            dma((CF,)),
            dma((4,)),
            dma((4,)),
            dma, dma((2,)), dma, dma((2,)), dma((2,)), dma,
            pltpu.SemaphoreType.REGULAR,
            pltpu.SemaphoreType.REGULAR,
        ],
        compiler_params=pltpu.CompilerParams(
            collective_id=0, has_side_effects=True, vmem_limit_bytes=40 * 1024 * 1024
        ),
    )(*(pltpu.with_memory_space_constraint(x, pltpu.HBM) for x in args))
    return pl.pallas_call(
        finish_kernel,
        out_shape=(pltpu.HBM(full, f32), pltpu.HBM(full, f32)),
        in_specs=[vmem] * 5,
        out_specs=(hbm, hbm),
        scratch_shapes=[V(full, f32), dma, dma((CF,))],
        compiler_params=pltpu.CompilerParams(vmem_limit_bytes=16 * 1024 * 1024),
    )(*(pltpu.with_memory_space_constraint(x, pltpu.VMEM) for x in parts))


def solution(mesh):
    in_specs = (
        P(None, "line", "blk", None),
        P(None, "line", "blk", None),
        P(),
        P(),
        P(),
        P("line", "blk", None),
        P(None, None, "line", "blk", None),
        P(None, "line", "blk", None),
        P(None, "line", "blk", None),
    )
    out_specs = (P(None, "line", "blk", None), P(None, "line", "blk", None))
    return jax.shard_map(local, mesh=mesh, in_specs=in_specs, out_specs=out_specs, check_vma=False)
```

```python
import jax
import jax.numpy as jnp
from jax import lax
from jax.experimental import pallas as pl
from jax.experimental.pallas import tpu as pltpu
from jax.sharding import PartitionSpec as P

F = 5
NV = 2 * F
CH = 2
UE = 4
UR = 8
US = 5
UB = 4
UF = 2
CF = 4
HALF = (slice(0, 8), slice(8, 16))
NXC = NYC = 4
SOLVERS = (
    ((3, 1), (12, 1), (9, 1), (5, 1), (13, 1), (6, 1), (8, 0), (7, 0), (0, 0), (4, 0)),
    ((0, 1), (4, 1), (12, 1), (15, 1), (3, 1), (8, 1), (1, 1), (2, 1), (11, 1), (7, 1)),
)
ORDER = (0, 1, 4, 3, 12, 2, 8, 5, 13, 7, 6, 9, 15, 14, 11, 10)


def planes(begin, count, unroll, body, carry, down=False):
    def one(z, carry):
        return body(begin - z if down else begin + z, carry)

    def some(i, carry):
        for j in range(unroll):
            carry = one(i * unroll + j, carry)
        return carry

    carry = lax.fori_loop(0, count // unroll, some, carry)
    for z in range(count - count % unroll, count):
        carry = one(z, carry)
    return carry


def tiles(fn):
    return tuple(fn(c, h) for c in range(F) for h in range(2))


def segment_kernel(
    visc_h, coup_h, thr_h, state_h, forcing_h, mask_h, binv_h, lower_h, upper_h,
    u0, rr, vv, fo, ret,
    st, mk, bi, lo, up, gl, gu, qg, pp, sw,
    visc, coup, thr, xs, xh, zh, low, acd_s, acd_r, be_s, be_r, ret_s, ret_r,
    small_sem, load_sem, binv_sem, halo_ssem, halo_rsem,
    acd_ssem, acd_rsem, be_ssem, be_rsem, ret_ssem, ret_rsem, row_sem, pair_sem,
):
    n_line = lax.axis_size("line")
    n_blk = lax.axis_size("blk")
    me = lax.axis_index("line")
    mb = lax.axis_index("blk")
    x, y, core = me // NYC, me % NYC, mb % 2
    depth = lo.shape[1]
    step = depth // CH
    half = depth // 2

    copy = pltpu.make_async_copy
    ld_state = copy(state_h, st.at[:, pl.ds(1, depth)], load_sem.at[0])
    ld_forcing = copy(forcing_h, fo, load_sem.at[1])
    ld_mask = copy(mask_h, mk, load_sem.at[2])
    ld_lower = copy(lower_h, lo, load_sem.at[3])
    ld_upper = copy(upper_h, up, load_sem.at[4])
    ld_small = [
        copy(src, dst, small_sem.at[i])
        for i, (src, dst) in enumerate(((visc_h, visc), (coup_h, coup), (thr_h, thr)))
    ]

    def ld_binv(k):
        part = pl.ds(k * step, step)
        return copy(binv_h.at[:, :, part], bi.at[:, :, part], binv_sem.at[k])

    ld_state.start()
    for cp in ld_small:
        cp.start()
    ld_lower.start()
    ld_upper.start()
    ld_forcing.start()
    ld_mask.start()

    has_low, has_high = me > 0, me < n_line - 1
    has_left, has_right = mb > 0, mb < n_blk - 1
    barrier = pltpu.get_barrier_semaphore()

    def greet(**device):
        pl.semaphore_signal(barrier, inc=1, device_id=device)

    def wrap(v, n):
        return jnp.where(v >= n, v - n, v)

    def in_column(d):
        return wrap(x + d, NXC) * NYC + y

    pl.when(has_left)(lambda: greet(blk=mb - 1))
    pl.when(has_right)(lambda: greet(blk=mb + 1))
    pl.when(has_low)(lambda: greet(line=me - 1))
    pl.when(has_high)(lambda: greet(line=me + 1))
    second = mb + 1 - core
    for d in range(1, NYC):
        greet(line=x * NYC + wrap(y + d, NYC), blk=second)

    @pl.when(core == 1)
    def _():
        for d in range(1, NXC):
            greet(line=in_column(d))

    for k in range(CH):
        ld_binv(k).start()

    zero_tile = jnp.zeros((8, 128), jnp.float32)
    one_tile = jnp.ones((8, 128), jnp.float32)
    for c in range(F):
        for sub in HALF:
            st[c, 0, sub, :] = zero_tile
            st[c, depth + 1, sub, :] = zero_tile
            sw[c, 0, sub, :] = zero_tile

    ld_state.wait()
    for c in range(F):
        for side, row in ((0, 0), (1, 15)):
            xs[side, c] = st[c, 1 : depth + 1, row, :]

    greeted = core * (2 * (NYC - 1) + NXC - 1)
    for cond in (has_left, has_right, has_low, has_high):
        greeted = greeted + jnp.where(cond, 1, 0)
    pl.semaphore_wait(barrier, greeted)

    def z_send(side):
        return pltpu.make_async_remote_copy(
            src_ref=st.at[:, depth if side else 1], dst_ref=zh.at[1 - side],
            send_sem=halo_ssem.at[side], recv_sem=halo_rsem.at[side],
            device_id={"line": me + 1 if side else me - 1},
        )

    def x_send(side, part):
        zs = pl.ds(part * half, half)
        return pltpu.make_async_remote_copy(
            src_ref=xs.at[side, :, zs], dst_ref=xh.at[1 - side, :, zs],
            send_sem=halo_ssem.at[2 + 2 * part + side], recv_sem=halo_rsem.at[2 + 2 * part + side],
            device_id={"blk": mb + 1 if side else mb - 1},
        )

    outgoing = (
        (has_low, z_send(0)),
        (has_high, z_send(1)),
        (has_left, x_send(0, 0)),
        (has_right, x_send(1, 0)),
        (has_left, x_send(0, 1)),
        (has_right, x_send(1, 1)),
    )
    for cond, out in outgoing:
        pl.when(cond)(out.start)

    @pl.when(core == 1)
    def _():
        for d in range(1, NXC):
            pl.semaphore_signal(row_sem, inc=1, device_id={"line": in_column(d)})

    ld_lower.wait()
    ld_upper.wait()
    for c in range(F):
        for h, sub in enumerate(HALF):
            low[c, h] = lo[c, 0, sub, :]
            lo[c, 0, sub, :] = one_tile


    def decay_plane(z, carry):
        new = []
        for i, (p, q, r) in enumerate(carry):
            c, sub = i // 2, HALF[i % 2]
            l, u = lo[c, z, sub, :], up[c, z, sub, :]
            l2 = 1.0 - l * l
            u2 = 1.0 - u * u
            g = u2 * lax.rsqrt(u2)
            gl[c, z, sub, :] = l2 * lax.rsqrt(l2)
            gu[c, z, sub, :] = g
            p = p * l
            w = q * g
            pp[c, z, sub, :] = p
            qg[c, z, sub, :] = w
            new.append((p, q * u, r + w * p))
        return tuple(new)

    acd = planes(0, depth, UE, decay_plane, ((one_tile, one_tile, zero_tile),) * NV)
    for c in range(F):
        for h, sub in enumerate(HALF):
            l2 = 1.0 - low[c, h] * low[c, h]
            gl[c, 0, sub, :] = l2 * lax.rsqrt(l2)
            p, q, r = acd[2 * c + h]
            acd_s[2 * c + h, 0] = p * low[c, h]
            acd_s[2 * c + h, 1] = q
            acd_s[2 * c + h, 2] = r * low[c, h]

    ld_forcing.wait()
    ld_mask.wait()
    for cp in ld_small:
        cp.wait()
    rows = lax.broadcasted_iota(jnp.int32, (8, 128), 0)
    first = rows == 0
    last = rows == 7
    vis = [visc[c] for c in range(F)]
    mat = [[-coup[c, d] for d in range(F)] for c in range(F)]
    plain = [mat[c][c] - 6.0 * vis[c] for c in range(F)]
    sunk = [plain[c] - thr[c] for c in range(F)]

    def residual_plane(z, carry):
        cen = [[st[c, z + 1, sub, :] for sub in HALF] for c in range(F)]
        disk = [mk[z, sub, :] != 0 for sub in HALF]
        for c in range(F):
            v0, v1 = cen[c]
            r0, r1 = pltpu.roll(v0, 1, 0), pltpu.roll(v1, 1, 0)
            q0, q1 = pltpu.roll(v0, 7, 0), pltpu.roll(v1, 7, 0)
            xsum = (
                jnp.where(first, 0.0, r0) + jnp.where(last, q1, q0),
                jnp.where(first, r0, r1) + jnp.where(last, 0.0, q1),
            )
            for h, sub in enumerate(HALF):
                v = cen[c][h]
                beside = (st[c, z, sub, :] + st[c, z + 2, sub, :]) + xsum[h]
                beside = beside + (pltpu.roll(v, 1, 1) + pltpu.roll(v, 127, 1))
                total = fo[c, z, sub, :] + vis[c] * beside
                total = total + jnp.where(disk[h], sunk[c], plain[c]) * v
                for d in range(F):
                    if d != c:
                        total = total + mat[c][d] * cen[d][h]
                fo[c, z, sub, :] = total
        return carry

    planes(0, depth // 2, UR, residual_plane, 0)

    other = mb + 1 - 2 * core

    @pl.when(core == 1)
    def _():
        pl.semaphore_wait(row_sem, NXC - 1)
        pl.semaphore_signal(pair_sem, inc=1, device_id={"blk": other})

    planes(depth // 2, depth // 2, UR, residual_plane, 0)

    @pl.when(core == 0)
    def _():
        pl.semaphore_wait(pair_sem, 1)


    def drain(ref, sem):
        copy(ref, ref, sem).wait()

    def to_solvers(src, dst, ssem, rsem):
        for mine in range(2):

            @pl.when(core == mine)
            def _():
                for v, (line, at) in enumerate(SOLVERS[mine]):
                    out = pltpu.make_async_remote_copy(
                        src_ref=src.at[v], dst_ref=dst.at[int(at == mine), me], send_sem=ssem,
                        recv_sem=rsem.at[int(at == mine)],
                        device_id={"line": line, "blk": mb if at == mine else other},
                    )
                    if at == mine:
                        pl.when(me != line)(out.start)
                    else:
                        out.start()

    to_solvers(acd_s, acd_r, acd_ssem, acd_rsem)

    def source(z, c, sub):
        src = bi[c, 0, z, sub, :] * fo[0, z, sub, :]
        for d in range(1, F):
            src = src + bi[c, d, z, sub, :] * fo[d, z, sub, :]
        return gl[c, z, sub, :] * src

    def sweep_plane(z, carry, sub):
        new = []
        for c, (s, e) in enumerate(carry):
            v = lo[c, z, sub, :] * s + source(z, c, sub)
            sw[c, z, sub, :] = v
            new.append((v, e + qg[c, z, sub, :] * v))
        return tuple(new)

    def add_x(side, part, row):
        zs = slice(part * half, part * half + half)
        for c in range(F):
            fo[c, zs, row, :] = fo[c, zs, row, :] + vis[c] * xh[side, c, zs]

    def add_z(side, z):
        for c in range(F):
            fo[c, z] = fo[c, z] + vis[c] * zh[side, c]

    def sweep_half(turn, unused):
        h = jnp.where(core == 1, turn, 1 - turn)
        sub = pl.ds(pl.multiple_of(8 * h, 8), 8)

        def x_halo(part):
            @pl.when(jnp.logical_and(h == 0, has_left))
            def _():
                x_send(1, part).wait_recv()
                add_x(0, part, 0)

            @pl.when(jnp.logical_and(h == 1, has_right))
            def _():
                x_send(0, part).wait_recv()
                add_x(1, part, 15)

        carry = ((zero_tile, zero_tile),) * F
        for k in range(CH):
            if k * step % half == 0:
                x_halo(k * step // half)
            pl.when(turn == 0)(ld_binv(k).wait)
            begin = max(k * step, 1)
            end = min((k + 1) * step, depth - 1)
            carry = planes(begin, end - begin, US, lambda z, c: sweep_plane(z, c, sub), carry)
        for c in range(F):
            be_s[2 * c + h, 0] = carry[c][0]
            be_s[2 * c + h, 1] = carry[c][1]
        return unused

    lax.fori_loop(0, 2, sweep_half, 0)

    @pl.when(has_high)
    def _():
        z_send(0).wait_recv()
        add_z(1, depth - 1)

    @pl.when(has_low)
    def _():
        z_send(1).wait_recv()
        add_z(0, 0)

    for h, sub in enumerate(HALF):
        carry = tuple((be_s[2 * c + h, 0], be_s[2 * c + h, 1]) for c in range(F))
        carry = sweep_plane(depth - 1, carry, sub)
        for c in range(F):
            p, q, r = acd[2 * c + h]
            s0 = source(0, c, sub)
            be_s[2 * c + h, 0] = carry[c][0] + p * s0
            be_s[2 * c + h, 1] = carry[c][1] + r * s0
            ret[c, h, 0] = s0
    to_solvers(be_s, be_r, be_ssem, be_rsem)

    def down_plane(z, carry):
        new = []
        for i, (u, r, v) in enumerate(carry):
            c, sub = i // 2, HALF[i % 2]
            a, g = up[c, z, sub, :], gu[c, z, sub, :]
            u = a * u + g * sw[c, z, sub, :]
            r = a * r + g * pp[c, z, sub, :]
            v = a * v
            u0[c, z, sub, :] = u
            rr[c, z, sub, :] = r
            vv[c, z, sub, :] = v
            new.append((u, r, v))
        return tuple(new)

    planes(depth - 1, depth, UB, down_plane, ((zero_tile, zero_tile, one_tile),) * NV, down=True)

    def role(cross):
        found, tile = False, 0
        for mine in range(2):
            for v, (line, at) in enumerate(SOLVERS[mine]):
                if (at != mine) == cross:
                    here = jnp.logical_and(core == at, me == line)
                    found = jnp.logical_or(found, here)
                    tile = jnp.where(here, v, tile)
        return found, tile

    def solve(tile, cross):
        i = 0 if cross else 1
        count = n_line if cross else n_line - 1
        if not cross:
            acd_r[i, me] = acd_s[tile]
            be_r[i, me] = be_s[tile]
        drain(acd_r.at[i, pl.ds(0, count)], acd_rsem.at[i])
        drain(be_r.at[i, pl.ds(0, count)], be_rsem.at[i])
        s = zero_tile
        t = []
        for k in range(n_line):
            ret_s[i, k, 0] = s
            t.append(acd_r[i, k, 2] * s + be_r[i, k, 1])
            s = acd_r[i, k, 0] * s + be_r[i, k, 0]
        u = zero_tile
        for k in range(n_line - 1, -1, -1):
            ret_s[i, k, 1] = u
            u = acd_r[i, k, 1] * u + t[k]
        for k in ORDER:
            out = pltpu.make_async_remote_copy(
                src_ref=ret_s.at[i, k], dst_ref=ret_r.at[tile], send_sem=ret_ssem.at[i], recv_sem=ret_rsem,
                device_id={"line": k, "blk": other if cross else mb},
            )
            if cross:
                out.start()
            else:
                pl.when(me != k)(out.start)
        if not cross:
            ret_r[tile] = ret_s[i, me]

    solves_other, other_tile = role(True)
    solves_own, own_tile = role(False)

    @pl.when(solves_own)
    def _():
        solve(own_tile, False)

    @pl.when(solves_other)
    def _():
        solve(other_tile, True)

    @pl.when(solves_own)
    def _():
        drain(ret_r.at[pl.ds(0, NV - 1)], ret_rsem)
        drain(acd_s.at[pl.ds(0, NV - 1)], acd_ssem)
        drain(be_s.at[pl.ds(0, NV - 1)], be_ssem)

    @pl.when(jnp.logical_not(solves_own))
    def _():
        drain(ret_r, ret_rsem)
        drain(acd_s, acd_ssem)
        drain(be_s, be_ssem)

    for c in range(F):
        for h in range(2):
            ret[c, h, 0] = ret[c, h, 0] + low[c, h] * ret_r[2 * c + h, 0]
            ret[c, h, 1] = ret_r[2 * c + h, 1]

    for cond, out in outgoing:
        pl.when(cond)(out.wait_send)
    pl.when(solves_other)(lambda: drain(ret_s.at[0], ret_ssem.at[0]))
    pl.when(solves_own)(lambda: drain(ret_s.at[1, pl.ds(0, n_line - 1)], ret_ssem.at[1]))


def finish_kernel(u0, rr, vv, fo, ret, update_h, resid_h, out, res_sem, out_sem):
    depth = u0.shape[1]
    step = depth // CF
    write_res = pltpu.make_async_copy(fo, resid_h, res_sem)
    write_res.start()

    def update_copy(k):
        part = pl.ds(k * step, step)
        return pltpu.make_async_copy(out.at[:, part], update_h.at[:, part], out_sem.at[k])

    s_in = tiles(lambda c, h: ret[c, h, 0])
    u_in = tiles(lambda c, h: ret[c, h, 1])

    def plane(z, carry):
        for i in range(NV):
            c, sub = i // 2, HALF[i % 2]
            out[c, z, sub, :] = u0[c, z, sub, :] + rr[c, z, sub, :] * s_in[i] + vv[c, z, sub, :] * u_in[i]
        return carry

    for k in range(CF):
        planes(k * step, step, UF, plane, 0)
        update_copy(k).start()
    write_res.wait()
    for k in range(CF):
        update_copy(k).wait()


def local(
    state, forcing, viscosity, coupling, thrust, disk_mask, block_inverse, lower_decay, upper_decay
):
    fields, depth, width, lanes = state.shape
    n_line = lax.axis_size("line")
    full = (fields, depth, width, lanes)
    f32 = jnp.float32
    V = pltpu.VMEM
    dma = pltpu.SemaphoreType.DMA
    hbm = pl.BlockSpec(memory_space=pltpu.HBM)
    vmem = pl.BlockSpec(memory_space=pltpu.VMEM)
    args = (viscosity, coupling, thrust, state, forcing, disk_mask, block_inverse, lower_decay, upper_decay)
    parts = pl.pallas_call(
        segment_kernel,
        out_shape=(V(full, f32),) * 4 + (V((fields, 2, 2, 8, lanes), f32),),
        in_specs=[hbm] * len(args),
        out_specs=(vmem,) * 5,
        scratch_shapes=[
            V((fields, depth + 2, width, lanes), f32),
            V((depth, width, lanes), jnp.int32),
            V((fields,) + full, f32),
            V(full, f32),
            V(full, f32),
            V(full, f32),
            V(full, f32),
            V(full, f32),
            V(full, f32),
            V(full, f32),
            pltpu.SMEM((fields,), f32),
            pltpu.SMEM((fields, fields), f32),
            pltpu.SMEM((fields,), f32),
            V((2, fields, depth, lanes), f32),
            V((2, fields, depth, lanes), f32),
            V((2, fields, width, lanes), f32),
            V((fields, 2, 8, lanes), f32),
            V((NV, 3, 8, lanes), f32),
            V((2, n_line, 3, 8, lanes), f32),
            V((NV, 2, 8, lanes), f32),
            V((2, n_line, 2, 8, lanes), f32),
            V((2, n_line, 2, 8, lanes), f32),
            V((NV, 2, 8, lanes), f32),
            dma((3,)),
            dma((5,)),
            dma((CF,)),
            dma((6,)),
            dma((6,)),
            dma, dma((2,)), dma, dma((2,)), dma((2,)), dma,
            pltpu.SemaphoreType.REGULAR,
            pltpu.SemaphoreType.REGULAR,
        ],
        compiler_params=pltpu.CompilerParams(
            collective_id=0, has_side_effects=True, vmem_limit_bytes=40 * 1024 * 1024
        ),
    )(*(pltpu.with_memory_space_constraint(x, pltpu.HBM) for x in args))
    return pl.pallas_call(
        finish_kernel,
        out_shape=(pltpu.HBM(full, f32), pltpu.HBM(full, f32)),
        in_specs=[vmem] * 5,
        out_specs=(hbm, hbm),
        scratch_shapes=[V(full, f32), dma, dma((CF,))],
        compiler_params=pltpu.CompilerParams(vmem_limit_bytes=16 * 1024 * 1024),
    )(*(pltpu.with_memory_space_constraint(x, pltpu.VMEM) for x in parts))


def solution(mesh):
    in_specs = (
        P(None, "line", "blk", None),
        P(None, "line", "blk", None),
        P(),
        P(),
        P(),
        P("line", "blk", None),
        P(None, None, "line", "blk", None),
        P(None, "line", "blk", None),
        P(None, "line", "blk", None),
    )
    out_specs = (P(None, "line", "blk", None), P(None, "line", "blk", None))
    return jax.shard_map(local, mesh=mesh, in_specs=in_specs, out_specs=out_specs, check_vma=False)
```

```python
import jax
import jax.numpy as jnp
from jax import lax
from jax.experimental import pallas as pl
from jax.experimental.pallas import tpu as pltpu
from jax.sharding import PartitionSpec as P

F = 5
NV = 2 * F
CH = 2
UE = 4
UR = 8
US = 5
UB = 4
UF = 2
CF = 4
HALF = (slice(0, 8), slice(8, 16))
NXC = NYC = 4
SOLVERS = (
    ((3, 1), (12, 1), (9, 1), (5, 1), (13, 1), (6, 1), (8, 0), (7, 0), (0, 0), (4, 0)),
    ((0, 1), (4, 1), (12, 1), (15, 1), (3, 1), (8, 1), (1, 1), (2, 1), (11, 1), (7, 1)),
)
ORDER = (0, 1, 4, 3, 12, 2, 8, 5, 13, 7, 6, 9, 15, 14, 11, 10)


def planes(begin, count, unroll, body, carry, down=False):
    def one(z, carry):
        return body(begin - z if down else begin + z, carry)

    def some(i, carry):
        for j in range(unroll):
            carry = one(i * unroll + j, carry)
        return carry

    carry = lax.fori_loop(0, count // unroll, some, carry)
    for z in range(count - count % unroll, count):
        carry = one(z, carry)
    return carry


def tiles(fn):
    return tuple(fn(c, h) for c in range(F) for h in range(2))


def segment_kernel(
    visc_h, coup_h, thr_h, state_h, forcing_h, mask_h, binv_h, lower_h, upper_h,
    u0, rr, vv, fo, ret,
    st, mk, bi, lo, up, gl, gu, qg, pp, sw,
    visc, coup, thr, xs, xh, zh, low, acd_s, acd_r, be_s, be_r, ret_s, ret_r,
    small_sem, load_sem, binv_sem, halo_ssem, halo_rsem,
    acd_ssem, acd_rsem, be_ssem, be_rsem, ret_ssem, ret_rsem, row_sem, pair_sem,
):
    n_line = lax.axis_size("line")
    n_blk = lax.axis_size("blk")
    me = lax.axis_index("line")
    mb = lax.axis_index("blk")
    x, y, core = me // NYC, me % NYC, mb % 2
    depth = lo.shape[1]
    step = depth // CH
    half = depth // 2

    copy = pltpu.make_async_copy
    ld_state = copy(state_h, st.at[:, pl.ds(1, depth)], load_sem.at[0])
    ld_forcing = copy(forcing_h, fo, load_sem.at[1])
    ld_mask = copy(mask_h, mk, load_sem.at[2])
    ld_lower = copy(lower_h, lo, load_sem.at[3])
    ld_upper = copy(upper_h, up, load_sem.at[4])
    ld_small = [
        copy(src, dst, small_sem.at[i])
        for i, (src, dst) in enumerate(((visc_h, visc), (coup_h, coup), (thr_h, thr)))
    ]

    def ld_binv(k):
        part = pl.ds(k * step, step)
        return copy(binv_h.at[:, :, part], bi.at[:, :, part], binv_sem.at[k])

    ld_state.start()
    for cp in ld_small:
        cp.start()
    ld_lower.start()
    ld_upper.start()
    ld_forcing.start()
    ld_mask.start()

    has_low, has_high = me > 0, me < n_line - 1
    has_left, has_right = mb > 0, mb < n_blk - 1
    barrier = pltpu.get_barrier_semaphore()

    def greet(**device):
        pl.semaphore_signal(barrier, inc=1, device_id=device)

    def wrap(v, n):
        return jnp.where(v >= n, v - n, v)

    def in_column(d):
        return wrap(x + d, NXC) * NYC + y

    pl.when(has_left)(lambda: greet(blk=mb - 1))
    pl.when(has_right)(lambda: greet(blk=mb + 1))
    pl.when(has_low)(lambda: greet(line=me - 1))
    pl.when(has_high)(lambda: greet(line=me + 1))
    second = mb + 1 - core
    for d in range(1, NYC):
        greet(line=x * NYC + wrap(y + d, NYC), blk=second)

    @pl.when(core == 1)
    def _():
        for d in range(1, NXC):
            greet(line=in_column(d))

    for k in range(CH):
        ld_binv(k).start()

    zero_tile = jnp.zeros((8, 128), jnp.float32)
    one_tile = jnp.ones((8, 128), jnp.float32)
    for c in range(F):
        for sub in HALF:
            st[c, 0, sub, :] = zero_tile
            st[c, depth + 1, sub, :] = zero_tile
            sw[c, 0, sub, :] = zero_tile

    ld_state.wait()
    for c in range(F):
        for side, row in ((0, 0), (1, 15)):
            xs[side, c] = st[c, 1 : depth + 1, row, :]

    greeted = core * (2 * (NYC - 1) + NXC - 1)
    for cond in (has_left, has_right, has_low, has_high):
        greeted = greeted + jnp.where(cond, 1, 0)
    pl.semaphore_wait(barrier, greeted)

    def z_send(side):
        return pltpu.make_async_remote_copy(
            src_ref=st.at[:, depth if side else 1], dst_ref=zh.at[1 - side],
            send_sem=halo_ssem.at[side], recv_sem=halo_rsem.at[side],
            device_id={"line": me + 1 if side else me - 1},
        )

    def x_send(side, part):
        zs = pl.ds(part * half, half)
        return pltpu.make_async_remote_copy(
            src_ref=xs.at[side, :, zs], dst_ref=xh.at[1 - side, :, zs],
            send_sem=halo_ssem.at[2 + 2 * part + side], recv_sem=halo_rsem.at[2 + 2 * part + side],
            device_id={"blk": mb + 1 if side else mb - 1},
        )

    outgoing = (
        (has_left, x_send(0, 0)),
        (has_right, x_send(1, 0)),
        (has_left, x_send(0, 1)),
        (has_right, x_send(1, 1)),
        (has_low, z_send(0)),
        (has_high, z_send(1)),
    )
    for cond, out in outgoing:
        pl.when(cond)(out.start)

    @pl.when(core == 1)
    def _():
        for d in range(1, NXC):
            pl.semaphore_signal(row_sem, inc=1, device_id={"line": in_column(d)})

    ld_lower.wait()
    ld_upper.wait()
    for c in range(F):
        for h, sub in enumerate(HALF):
            low[c, h] = lo[c, 0, sub, :]
            lo[c, 0, sub, :] = one_tile


    def decay_plane(z, carry):
        new = []
        for i, (p, q, r) in enumerate(carry):
            c, sub = i // 2, HALF[i % 2]
            l, u = lo[c, z, sub, :], up[c, z, sub, :]
            l2 = 1.0 - l * l
            u2 = 1.0 - u * u
            g = u2 * lax.rsqrt(u2)
            gl[c, z, sub, :] = l2 * lax.rsqrt(l2)
            gu[c, z, sub, :] = g
            p = p * l
            w = q * g
            pp[c, z, sub, :] = p
            qg[c, z, sub, :] = w
            new.append((p, q * u, r + w * p))
        return tuple(new)

    acd = planes(0, depth, UE, decay_plane, ((one_tile, one_tile, zero_tile),) * NV)
    for c in range(F):
        for h, sub in enumerate(HALF):
            l2 = 1.0 - low[c, h] * low[c, h]
            gl[c, 0, sub, :] = l2 * lax.rsqrt(l2)
            p, q, r = acd[2 * c + h]
            acd_s[2 * c + h, 0] = p * low[c, h]
            acd_s[2 * c + h, 1] = q
            acd_s[2 * c + h, 2] = r * low[c, h]

    ld_forcing.wait()
    ld_mask.wait()
    for cp in ld_small:
        cp.wait()
    rows = lax.broadcasted_iota(jnp.int32, (8, 128), 0)
    first = rows == 0
    last = rows == 7
    vis = [visc[c] for c in range(F)]
    mat = [[-coup[c, d] for d in range(F)] for c in range(F)]
    plain = [mat[c][c] - 6.0 * vis[c] for c in range(F)]
    sunk = [plain[c] - thr[c] for c in range(F)]

    def residual_plane(z, carry):
        cen = [[st[c, z + 1, sub, :] for sub in HALF] for c in range(F)]
        disk = [mk[z, sub, :] != 0 for sub in HALF]
        for c in range(F):
            v0, v1 = cen[c]
            r0, r1 = pltpu.roll(v0, 1, 0), pltpu.roll(v1, 1, 0)
            q0, q1 = pltpu.roll(v0, 7, 0), pltpu.roll(v1, 7, 0)
            xsum = (
                jnp.where(first, 0.0, r0) + jnp.where(last, q1, q0),
                jnp.where(first, r0, r1) + jnp.where(last, 0.0, q1),
            )
            for h, sub in enumerate(HALF):
                v = cen[c][h]
                beside = (st[c, z, sub, :] + st[c, z + 2, sub, :]) + xsum[h]
                beside = beside + (pltpu.roll(v, 1, 1) + pltpu.roll(v, 127, 1))
                total = fo[c, z, sub, :] + vis[c] * beside
                total = total + jnp.where(disk[h], sunk[c], plain[c]) * v
                for d in range(F):
                    if d != c:
                        total = total + mat[c][d] * cen[d][h]
                fo[c, z, sub, :] = total
        return carry

    planes(0, depth // 2, UR, residual_plane, 0)

    other = mb + 1 - 2 * core

    @pl.when(core == 1)
    def _():
        pl.semaphore_wait(row_sem, NXC - 1)
        pl.semaphore_signal(pair_sem, inc=1, device_id={"blk": other})

    planes(depth // 2, depth // 2, UR, residual_plane, 0)

    @pl.when(core == 0)
    def _():
        pl.semaphore_wait(pair_sem, 1)


    def drain(ref, sem):
        copy(ref, ref, sem).wait()

    def to_solvers(src, dst, ssem, rsem):
        for mine in range(2):

            @pl.when(core == mine)
            def _():
                for v, (line, at) in enumerate(SOLVERS[mine]):
                    out = pltpu.make_async_remote_copy(
                        src_ref=src.at[v], dst_ref=dst.at[int(at == mine), me], send_sem=ssem,
                        recv_sem=rsem.at[int(at == mine)],
                        device_id={"line": line, "blk": mb if at == mine else other},
                    )
                    if at == mine:
                        pl.when(me != line)(out.start)
                    else:
                        out.start()

    to_solvers(acd_s, acd_r, acd_ssem, acd_rsem)

    def source(z, c, sub):
        src = bi[c, 0, z, sub, :] * fo[0, z, sub, :]
        for d in range(1, F):
            src = src + bi[c, d, z, sub, :] * fo[d, z, sub, :]
        return gl[c, z, sub, :] * src

    def sweep_plane(z, carry, sub):
        new = []
        for c, (s, e) in enumerate(carry):
            v = lo[c, z, sub, :] * s + source(z, c, sub)
            sw[c, z, sub, :] = v
            new.append((v, e + qg[c, z, sub, :] * v))
        return tuple(new)

    def add_x(side, part, row):
        zs = slice(part * half, part * half + half)
        for c in range(F):
            fo[c, zs, row, :] = fo[c, zs, row, :] + vis[c] * xh[side, c, zs]

    def add_z(side, z):
        for c in range(F):
            fo[c, z] = fo[c, z] + vis[c] * zh[side, c]

    def sweep_half(turn, unused):
        h = jnp.where(core == 1, turn, 1 - turn)
        sub = pl.ds(pl.multiple_of(8 * h, 8), 8)

        def x_halo(part):
            @pl.when(jnp.logical_and(h == 0, has_left))
            def _():
                x_send(1, part).wait_recv()
                add_x(0, part, 0)

            @pl.when(jnp.logical_and(h == 1, has_right))
            def _():
                x_send(0, part).wait_recv()
                add_x(1, part, 15)

        carry = ((zero_tile, zero_tile),) * F
        for k in range(CH):
            if k * step % half == 0:
                x_halo(k * step // half)
            pl.when(turn == 0)(ld_binv(k).wait)
            begin = max(k * step, 1)
            end = min((k + 1) * step, depth - 1)
            carry = planes(begin, end - begin, US, lambda z, c: sweep_plane(z, c, sub), carry)
        for c in range(F):
            be_s[2 * c + h, 0] = carry[c][0]
            be_s[2 * c + h, 1] = carry[c][1]
        return unused

    lax.fori_loop(0, 2, sweep_half, 0)

    @pl.when(has_high)
    def _():
        z_send(0).wait_recv()
        add_z(1, depth - 1)

    @pl.when(has_low)
    def _():
        z_send(1).wait_recv()
        add_z(0, 0)

    for h, sub in enumerate(HALF):
        carry = tuple((be_s[2 * c + h, 0], be_s[2 * c + h, 1]) for c in range(F))
        carry = sweep_plane(depth - 1, carry, sub)
        for c in range(F):
            p, q, r = acd[2 * c + h]
            s0 = source(0, c, sub)
            be_s[2 * c + h, 0] = carry[c][0] + p * s0
            be_s[2 * c + h, 1] = carry[c][1] + r * s0
            ret[c, h, 0] = s0
    to_solvers(be_s, be_r, be_ssem, be_rsem)

    def down_plane(z, carry):
        new = []
        for i, (u, r, v) in enumerate(carry):
            c, sub = i // 2, HALF[i % 2]
            a, g = up[c, z, sub, :], gu[c, z, sub, :]
            u = a * u + g * sw[c, z, sub, :]
            r = a * r + g * pp[c, z, sub, :]
            v = a * v
            u0[c, z, sub, :] = u
            rr[c, z, sub, :] = r
            vv[c, z, sub, :] = v
            new.append((u, r, v))
        return tuple(new)

    planes(depth - 1, depth, UB, down_plane, ((zero_tile, zero_tile, one_tile),) * NV, down=True)

    def role(cross):
        found, tile = False, 0
        for mine in range(2):
            for v, (line, at) in enumerate(SOLVERS[mine]):
                if (at != mine) == cross:
                    here = jnp.logical_and(core == at, me == line)
                    found = jnp.logical_or(found, here)
                    tile = jnp.where(here, v, tile)
        return found, tile

    def solve(tile, cross):
        i = 0 if cross else 1
        count = n_line if cross else n_line - 1
        if not cross:
            acd_r[i, me] = acd_s[tile]
            be_r[i, me] = be_s[tile]
        drain(acd_r.at[i, pl.ds(0, count)], acd_rsem.at[i])
        drain(be_r.at[i, pl.ds(0, count)], be_rsem.at[i])
        s = zero_tile
        t = []
        for k in range(n_line):
            ret_s[i, k, 0] = s
            t.append(acd_r[i, k, 2] * s + be_r[i, k, 1])
            s = acd_r[i, k, 0] * s + be_r[i, k, 0]
        u = zero_tile
        for k in range(n_line - 1, -1, -1):
            ret_s[i, k, 1] = u
            u = acd_r[i, k, 1] * u + t[k]
        for k in ORDER:
            out = pltpu.make_async_remote_copy(
                src_ref=ret_s.at[i, k], dst_ref=ret_r.at[tile], send_sem=ret_ssem.at[i], recv_sem=ret_rsem,
                device_id={"line": k, "blk": other if cross else mb},
            )
            if cross:
                out.start()
            else:
                pl.when(me != k)(out.start)
        if not cross:
            ret_r[tile] = ret_s[i, me]

    solves_other, other_tile = role(True)
    solves_own, own_tile = role(False)

    @pl.when(solves_own)
    def _():
        solve(own_tile, False)

    @pl.when(solves_other)
    def _():
        solve(other_tile, True)

    @pl.when(solves_own)
    def _():
        drain(ret_r.at[pl.ds(0, NV - 1)], ret_rsem)
        drain(acd_s.at[pl.ds(0, NV - 1)], acd_ssem)
        drain(be_s.at[pl.ds(0, NV - 1)], be_ssem)

    @pl.when(jnp.logical_not(solves_own))
    def _():
        drain(ret_r, ret_rsem)
        drain(acd_s, acd_ssem)
        drain(be_s, be_ssem)

    for c in range(F):
        for h in range(2):
            ret[c, h, 0] = ret[c, h, 0] + low[c, h] * ret_r[2 * c + h, 0]
            ret[c, h, 1] = ret_r[2 * c + h, 1]

    for cond, out in outgoing:
        pl.when(cond)(out.wait_send)
    pl.when(solves_other)(lambda: drain(ret_s.at[0], ret_ssem.at[0]))
    pl.when(solves_own)(lambda: drain(ret_s.at[1, pl.ds(0, n_line - 1)], ret_ssem.at[1]))


def finish_kernel(u0, rr, vv, fo, ret, update_h, resid_h, out, res_sem, out_sem):
    depth = u0.shape[1]
    step = depth // CF
    write_res = pltpu.make_async_copy(fo, resid_h, res_sem)
    write_res.start()

    def update_copy(k):
        part = pl.ds(k * step, step)
        return pltpu.make_async_copy(out.at[:, part], update_h.at[:, part], out_sem.at[k])

    s_in = tiles(lambda c, h: ret[c, h, 0])
    u_in = tiles(lambda c, h: ret[c, h, 1])

    def plane(z, carry):
        for i in range(NV):
            c, sub = i // 2, HALF[i % 2]
            out[c, z, sub, :] = u0[c, z, sub, :] + rr[c, z, sub, :] * s_in[i] + vv[c, z, sub, :] * u_in[i]
        return carry

    for k in range(CF):
        planes(k * step, step, UF, plane, 0)
        update_copy(k).start()
    write_res.wait()
    for k in range(CF):
        update_copy(k).wait()


def local(
    state, forcing, viscosity, coupling, thrust, disk_mask, block_inverse, lower_decay, upper_decay
):
    fields, depth, width, lanes = state.shape
    n_line = lax.axis_size("line")
    full = (fields, depth, width, lanes)
    f32 = jnp.float32
    V = pltpu.VMEM
    dma = pltpu.SemaphoreType.DMA
    hbm = pl.BlockSpec(memory_space=pltpu.HBM)
    vmem = pl.BlockSpec(memory_space=pltpu.VMEM)
    args = (viscosity, coupling, thrust, state, forcing, disk_mask, block_inverse, lower_decay, upper_decay)
    parts = pl.pallas_call(
        segment_kernel,
        out_shape=(V(full, f32),) * 4 + (V((fields, 2, 2, 8, lanes), f32),),
        in_specs=[hbm] * len(args),
        out_specs=(vmem,) * 5,
        scratch_shapes=[
            V((fields, depth + 2, width, lanes), f32),
            V((depth, width, lanes), jnp.int32),
            V((fields,) + full, f32),
            V(full, f32),
            V(full, f32),
            V(full, f32),
            V(full, f32),
            V(full, f32),
            V(full, f32),
            V(full, f32),
            pltpu.SMEM((fields,), f32),
            pltpu.SMEM((fields, fields), f32),
            pltpu.SMEM((fields,), f32),
            V((2, fields, depth, lanes), f32),
            V((2, fields, depth, lanes), f32),
            V((2, fields, width, lanes), f32),
            V((fields, 2, 8, lanes), f32),
            V((NV, 3, 8, lanes), f32),
            V((2, n_line, 3, 8, lanes), f32),
            V((NV, 2, 8, lanes), f32),
            V((2, n_line, 2, 8, lanes), f32),
            V((2, n_line, 2, 8, lanes), f32),
            V((NV, 2, 8, lanes), f32),
            dma((3,)),
            dma((5,)),
            dma((CF,)),
            dma((6,)),
            dma((6,)),
            dma, dma((2,)), dma, dma((2,)), dma((2,)), dma,
            pltpu.SemaphoreType.REGULAR,
            pltpu.SemaphoreType.REGULAR,
        ],
        compiler_params=pltpu.CompilerParams(
            collective_id=0, has_side_effects=True, vmem_limit_bytes=40 * 1024 * 1024
        ),
    )(*(pltpu.with_memory_space_constraint(x, pltpu.HBM) for x in args))
    return pl.pallas_call(
        finish_kernel,
        out_shape=(pltpu.HBM(full, f32), pltpu.HBM(full, f32)),
        in_specs=[vmem] * 5,
        out_specs=(hbm, hbm),
        scratch_shapes=[V(full, f32), dma, dma((CF,))],
        compiler_params=pltpu.CompilerParams(vmem_limit_bytes=16 * 1024 * 1024),
    )(*(pltpu.with_memory_space_constraint(x, pltpu.VMEM) for x in parts))


def solution(mesh):
    in_specs = (
        P(None, "line", "blk", None),
        P(None, "line", "blk", None),
        P(),
        P(),
        P(),
        P("line", "blk", None),
        P(None, None, "line", "blk", None),
        P(None, "line", "blk", None),
        P(None, "line", "blk", None),
    )
    out_specs = (P(None, "line", "blk", None), P(None, "line", "blk", None))
    return jax.shard_map(local, mesh=mesh, in_specs=in_specs, out_specs=out_specs, check_vma=False)
```
